32 devices in a mesh: dp: 4 (over y, x), row: 4 (over z), col: 2 (over core).
Axes of the slice: x: 2, y: 2, z: 4, core: 2. Of those that a mesh axis runs over, the one named last changes fastest.
Arguments:
- inputs: bfloat16 [576, 16384], P('row', ('dp', 'col')), may hold values from -6 to 6
- cotangent: bfloat16 [576, 16384], P('row', ('dp', 'col')), may hold values from -6 to 6
- segments: int32 [16384], P(('dp', 'row')), may hold values from 0 to 2, as said below
- positions: int32 [16384], P(('dp', 'row')), may hold values from 0 to 1021, as said below
- attn_gain: float32 [2, 576], P(None, 'row'), may hold values from 0.5 to 1.5
- w_query: bfloat16 [2, 576, 576], P(None, 'row', 'col'), may hold values from -0.25 to 0.25
- w_key: bfloat16 [2, 576, 192], P(None, 'row', 'col'), may hold values from -0.25 to 0.25
- w_value: bfloat16 [2, 576, 192], P(None, 'row', 'col'), may hold values from -0.25 to 0.25
- w_out: bfloat16 [2, 576, 576], P(None, 'col', 'row'), may hold values from -2 to 2
- ff_gain: float32 [2, 576], P(None, 'row'), may hold values from 0.5 to 1.5
- w_gate: bfloat16 [2, 576, 1536], P(None, 'row', 'col'), may hold values from -0.25 to 0.25
- w_up: bfloat16 [2, 576, 1536], P(None, 'row', 'col'), may hold values from -0.25 to 0.25
- w_down: bfloat16 [2, 1536, 576], P(None, 'col', 'row'), may hold values from -0.15625 to 0.15625
Outputs:
- outputs: bfloat16 [576, 16384], P('row', ('dp', 'col'))
- input_grad: float32 [576, 16384], P('row', ('dp', 'col'))
- attn_gain_grad: float32 [2, 576], P(None, 'row')
- query_grad: float32 [2, 576, 576], P(None, 'row', 'col')
- key_grad: float32 [2, 576, 192], P(None, 'row', 'col')
- value_grad: float32 [2, 576, 192], P(None, 'row', 'col')
- out_grad: float32 [2, 576, 576], P(None, 'col', 'row')
- ff_gain_grad: float32 [2, 576], P(None, 'row')
- gate_grad: float32 [2, 576, 1536], P(None, 'row', 'col')
- up_grad: float32 [2, 576, 1536], P(None, 'row', 'col')
- down_grad: float32 [2, 1536, 576], P(None, 'col', 'row')
The draws below stay inside these ranges and needn't reach their ends.
Inputs may be any that keep to these rules, and one draw needn't show every extreme that they name: `segments`: segment numbers count documents within each sequence of 1024 consecutive tokens and never fall there; every sequence holds three documents, the first and the last with 1 to 256 tokens. `positions`: the position of a token within its document: 0 at each document's first token, rising by one.
All inputs are finite; a program needn't handle non-finite values.
Results may differ from the reference program's by a relative error of at most 0.02.
Values may be sent and summed in bfloat16 or wider, within the bound.
No kernel may reach another device: no remote copies, remote signals or barrier semaphores. Data moves between devices by JAX's collectives and lax.ppermute only.
A program may use at most 640 MiB of HBM per device.

```python
import jax
import jax.numpy as jnp
from jax import lax

D = 576
FF = 1536
H = 9
KVH = 3
HD = 64
LAYERS = 2
TOK_DEV = 512
Q = 576
KV = 192
SEQ = 1024
TOKENS = 16384


def sequence_layout(key):
    seq_count = TOKENS // SEQ
    key_first, key_second = jax.random.split(key)
    key_pick = jax.random.fold_in(key, 7)
    first = jax.random.randint(key_first, (seq_count, 1), 1, TOK_DEV // 2 + 1)
    second = SEQ - jax.random.randint(key_second, (seq_count, 1), 1, TOK_DEV // 2 + 1)
    picked = jax.random.randint(key_pick, (), 0, seq_count)
    chosen = jnp.arange(seq_count, dtype=jnp.int32)[:, None] == picked
    first = jnp.where(chosen, 1, first)
    second = jnp.where(chosen, SEQ - 1, second)
    places = jnp.arange(SEQ, dtype=jnp.int32)[None, :]
    segment = (places >= first).astype(jnp.int32) + (places >= second).astype(jnp.int32)
    starts = jnp.where(places >= second, second, jnp.where(places >= first, first, 0))
    return (segment.reshape(TOKENS), (places - starts).reshape(TOKENS))


def draw_segments(key, part):
    return sequence_layout(key)[0]


def draw_positions(key, part):
    return sequence_layout(key)[1]


def steps_of(own_key, shape, cuts, low, high):
    def one(position, parts):
        heights = jax.random.uniform(jax.random.fold_in(jax.random.fold_in(own_key, 6), position), (parts,), jnp.float32, low / len(cuts), high / len(cuts))
        return jnp.repeat(jnp.exp(heights), shape[position] // parts).reshape((-1,) + (1,) * (len(shape) - position - 1))

    factor_of = one(*cuts[0])
    for cut in cuts[1:]:
        factor_of = factor_of * one(*cut)
    return factor_of


def noise(key, shape, spread, reach, cuts=(), kind=jnp.bfloat16):
    drawn = jax.random.normal(key, shape, jnp.float32) * spread
    if len(cuts) > 0:
        drawn = steps_of(key, shape, cuts, -0.22, 0.18) * drawn
    return jnp.clip(drawn, min=-reach, max=reach).astype(kind)


def setup_inputs(seed: int = 0) -> dict:
    seeds = jax.random.split(jax.random.key(seed), 14)
    return {
        "inputs": noise(seeds[0], (D, TOKENS), 1.0, 6.0, ((0, 4), (1, 8))),
        "cotangent": noise(seeds[1], (D, TOKENS), 1.0, 6.0, ((0, 4), (1, 8))),
        "segments": draw_segments(jax.random.fold_in(seeds[13], 71), 0),
        "positions": draw_positions(jax.random.fold_in(seeds[13], 71), 0),
        "attn_gain": jnp.clip(1.0 + 0.1 * jax.random.normal(seeds[4], (LAYERS, D), jnp.float32), 0.5, 1.5),
        "w_query": noise(seeds[5], (LAYERS, D, Q), D ** -0.5, 0.25, ((1, 4), (2, 2))),
        "w_key": noise(seeds[6], (LAYERS, D, KV), D ** -0.5, 0.25, ((1, 4), (2, 2))),
        "w_value": noise(seeds[7], (LAYERS, D, KV), D ** -0.5, 0.25, ((1, 4), (2, 2))),
        "w_out": noise(seeds[8], (LAYERS, Q, D), (max(Q // 64, 1)) ** -0.5, 2.0, ((1, 2), (2, 4))),
        "ff_gain": jnp.clip(1.0 + 0.1 * jax.random.normal(seeds[9], (LAYERS, D), jnp.float32), 0.5, 1.5),
        "w_gate": noise(seeds[10], (LAYERS, D, FF), D ** -0.5, 0.25, ((1, 4), (2, 2))),
        "w_up": noise(seeds[11], (LAYERS, D, FF), D ** -0.5, 0.25, ((1, 4), (2, 2))),
        "w_down": noise(seeds[12], (LAYERS, FF, D), FF ** -0.5, 0.15625, ((1, 2), (2, 4))),
    }


EPSILON = 1e-05
ROTARY_BASE = 100000.0
NEGATIVE = -1e+30

@jax.custom_vjp
def low(v):
    return lax.optimization_barrier(v.astype(jnp.bfloat16)).astype(jnp.float32)

@jax.custom_vjp
def low_back(v):
    return v

def low_keep(v):
    return (low(v), None)

def low_pass(kept, grad):
    return (grad,)

def back_keep(v):
    return (v, None)

def back_low(kept, grad):
    return (low(grad),)
low.defvjp(low_keep, low_pass)
low_back.defvjp(back_keep, back_low)

def rounded_both(value):
    return low_back(low(value))

def product(left, right):
    return jnp.dot(left, right, precision=lax.Precision.HIGHEST)

def rms_norm(hidden, gain):
    return hidden * lax.rsqrt(lax.optimization_barrier(jnp.mean(hidden * hidden, axis=-1, keepdims=True)) + EPSILON) * gain

def rotary(values, places, head_count):
    half_dim = HD // 2
    frequency = ROTARY_BASE ** (-(jnp.arange(half_dim).astype(jnp.float32) / half_dim))
    angles = places.astype(jnp.float32)[:, None] * frequency[None, :]
    cosine = jnp.cos(angles)[:, None, :]
    sine_part = jnp.sin(angles)[:, None, :]
    shaped = values.reshape(values.shape[0], head_count, HD)
    first = shaped[..., :half_dim]
    second = shaped[..., half_dim:]
    turned = jnp.concatenate([first * cosine - second * sine_part, second * cosine + first * sine_part], axis=-1)
    return turned.reshape(values.shape[0], head_count * HD)

def attend_sequence(pieces):
    queries, keys, values, segment = pieces
    group_size = H // KVH
    key_heads = keys.reshape(SEQ, KVH, HD)
    value_heads = values.reshape(SEQ, KVH, HD)
    key_place = jnp.arange(SEQ, dtype=jnp.int32)

    def query_block(number):
        offset = (number * TOK_DEV).astype(jnp.int32)
        block_queries = lax.dynamic_slice_in_dim(queries, offset, TOK_DEV, 0).reshape(TOK_DEV, KVH, group_size, HD)
        query_segment = lax.dynamic_slice_in_dim(segment, offset, TOK_DEV, 0)
        query_place = offset + jnp.arange(TOK_DEV, dtype=jnp.int32)
        scores = jnp.einsum('qkgd,tkd->kgqt', block_queries, key_heads, precision=lax.Precision.HIGHEST)
        scores = low_back(scores * HD ** (-0.5))
        allowed = (query_segment[:, None] == segment[None, :]) & (query_place[:, None] >= key_place[None, :])
        scores = jnp.where(allowed[None, None], scores, NEGATIVE)
        largest = lax.optimization_barrier(jnp.max(scores, axis=-1, keepdims=True))
        weights = jnp.exp(scores - largest)
        weights = low(weights / lax.optimization_barrier(jnp.sum(weights, axis=-1, keepdims=True)))
        mixture = jnp.einsum('kgqt,tkd->qkgd', weights, value_heads, precision=lax.Precision.HIGHEST)
        return mixture.reshape(TOK_DEV, H * HD)
    blocks = lax.map(jax.checkpoint(query_block), jnp.arange(SEQ // TOK_DEV, dtype=jnp.int32))
    return blocks.reshape(SEQ, H * HD)

def layer_forward(hidden, segments, positions, gain_a, query_w, key_w, value_w, out_w, gain_f, gate_w, up_w, down_w):
    normed = low(rms_norm(hidden, gain_a))
    queries = low(rotary(rounded_both(product(normed, query_w)), positions, H))
    keys = low(rotary(rounded_both(product(normed, key_w)), positions, KVH))
    values = rounded_both(product(normed, value_w))
    seq_count = TOKENS // SEQ
    mixture = lax.map(attend_sequence, (queries.reshape(seq_count, SEQ, H * HD), keys.reshape(seq_count, SEQ, KVH * HD), values.reshape(seq_count, SEQ, KVH * HD), segments.reshape(seq_count, SEQ)))
    mixed = rounded_both(mixture.reshape(TOKENS, H * HD))
    middle = hidden + low_back(product(mixed, out_w))
    normed_f = low(rms_norm(middle, gain_f))
    gate_act = low_back(product(normed_f, gate_w))
    up_part = low_back(product(normed_f, up_w))
    inner_act = low(jax.nn.silu(gate_act) * up_part)
    return middle + low_back(product(inner_act, down_w))

def reference(inputs, cotangent, segments, positions, attn_gain, w_query, w_key, w_value, w_out, ff_gain, w_gate, w_up, w_down):
    params = tuple((array.astype(jnp.float32) for array in (attn_gain, w_query, w_key, w_value, w_out, ff_gain, w_gate, w_up, w_down)))

    def forward(initial, gain_a, query_w, key_w, value_w, out_w, gain_f, gate_w, up_w, down_w):
        hidden = initial
        for number in range(LAYERS):
            hidden = layer_forward(hidden, segments, positions, gain_a[number], query_w[number], key_w[number], value_w[number], out_w[number], gain_f[number], gate_w[number], up_w[number], down_w[number])
        return hidden
    result, pullback = jax.vjp(forward, inputs.astype(jnp.float32).T, *params)
    grads = pullback(cotangent.astype(jnp.float32).T)
    return (result.astype(jnp.bfloat16).T, grads[0].T, grads[1], grads[2], grads[3], grads[4], grads[5], grads[6], grads[7], grads[8], grads[9])
```

```python
import functools

import jax
import jax.numpy as jnp
from jax import lax
from jax.experimental import pallas as pl
from jax.experimental.pallas import tpu as pltpu
from jax.sharding import PartitionSpec as P

D = 576
H = 9
KVH = 3
HD = 64
GROUP = H // KVH

EPSILON = 1e-05
ROTARY_BASE = 100000.0
NEGATIVE = -1e30
BF = jnp.bfloat16
F32 = jnp.float32

ORDER = ((0, 3, 1, 2), (1, 2, 0, 3))
REACH = ((((0, 1),), ((0, 4),)), (((0, 1), (2, 3)), ((0, 3),)))

def mm(left, right, left_dim, right_dim):
    return lax.dot_general(left, right, (((left_dim,), (right_dim,)), ((), ())), preferred_element_type=F32)

def fill_bias(core, start_ref, bias_ref, quarter):
    for block in range(2):
        cols = slice(block * quarter, (block + 1) * quarter)
        query_place = lax.broadcasted_iota(jnp.int32, (quarter, quarter), 1) + ORDER[core][block] * quarter
        for begin, end in REACH[core][block]:
            for part in range(begin, end):
                key_place = lax.broadcasted_iota(jnp.int32, (quarter, quarter), 0) + ORDER[core][part] * quarter
                allowed = (key_place <= query_place) & (key_place >= start_ref[:, cols])
                bias_ref[part * quarter : (part + 1) * quarter, cols] = jnp.where(allowed, 0.0, NEGATIVE)

def forward_kernel(core_ref, start_ref, query_ref, key_ref, value_ref, mixture_ref, mixed_ref, total_ref, bias_ref, turned_ref):
    quarter = query_ref.shape[1] // 2
    turned_ref[...] = key_ref[...].T

    def branch(core):
        @pl.when(pl.program_id(0) == 0)
        def _():
            fill_bias(core, start_ref, bias_ref, quarter)

        def head(number, carry):
            rows = pl.ds(number * HD, HD)
            for block in range(2):
                cols = slice(block * quarter, (block + 1) * quarter)
                query = query_ref[rows, cols]
                spans = [slice(b * quarter, e * quarter) for b, e in REACH[core][block]]
                scores = [mm(turned_ref[span, :], query, 1, 0) + bias_ref[span, cols] for span in spans]
                largest = functools.reduce(jnp.maximum, [jnp.max(s, axis=0, keepdims=True) for s in scores])
                raised = [jnp.exp(s - largest) for s in scores]
                total = sum(jnp.sum(r, axis=0, keepdims=True) for r in raised)
                mixture = sum(mm(value_ref[:, span], r.astype(BF), 1, 0) for span, r in zip(spans, raised))
                mixture = mixture / total
                mixture_ref[rows, cols] = mixture
                mixed_ref[rows, cols] = mixture.astype(BF)
                total_ref[pl.ds(number, 1), cols] = largest + jnp.log(total)
            return carry
        lax.fori_loop(0, GROUP, head, 0)

    pl.when(core_ref[0] == 0)(lambda: branch(0))
    pl.when(core_ref[0] != 0)(lambda: branch(1))

def attend(core, starts, query, key_values):
    tokens = query.shape[1]
    spec = lambda rows, count: pl.BlockSpec((rows, count), lambda g, c: (g, 0))
    return pl.pallas_call(
        forward_kernel,
        out_shape=(jax.ShapeDtypeStruct((H * HD, tokens), F32), jax.ShapeDtypeStruct((H * HD, tokens), BF), jax.ShapeDtypeStruct((KVH, 8, tokens), F32)),
        grid_spec=pltpu.PrefetchScalarGridSpec(
            num_scalar_prefetch=1, grid=(KVH,),
            in_specs=[pl.BlockSpec((1, tokens), lambda g, c: (0, 0)), spec(GROUP * HD, tokens), spec(HD, 2 * tokens),
                      pl.BlockSpec((HD, 2 * tokens), lambda g, c: (g + KVH, 0))],
            out_specs=[spec(GROUP * HD, tokens), spec(GROUP * HD, tokens), pl.BlockSpec((None, 8, tokens), lambda g, c: (g, 0, 0))],
            scratch_shapes=[pltpu.VMEM((2 * tokens, tokens), F32), pltpu.VMEM((2 * tokens, HD), BF)],
        ),
        compiler_params=pltpu.CompilerParams(vmem_limit_bytes=40 * 2**20),
        cost_estimate=pl.CostEstimate(flops=4 * H * HD * 2 * tokens * tokens, bytes_accessed=8 * H * HD * tokens, transcendentals=H * tokens * tokens),
        name="attend",
    )(core, starts, query, key_values, key_values)

def backward_kernel(core_ref, start_ref, query_ref, key_ref, value_ref, grad_ref, mixture_ref, total_ref,
                    grad_query_ref, grad_key_ref, grad_value_ref, bias_ref, turned_key_ref, turned_value_ref):
    quarter = query_ref.shape[1] // 2
    turned_key_ref[...] = key_ref[...].T
    turned_value_ref[...] = value_ref[...].T
    grad_key_ref[...] = jnp.zeros_like(grad_key_ref)
    grad_value_ref[...] = jnp.zeros_like(grad_value_ref)

    def branch(core):
        @pl.when(pl.program_id(0) == 0)
        def _():
            fill_bias(core, start_ref, bias_ref, quarter)

        def head(number, carry):
            rows = pl.ds(number * HD, HD)
            for block in range(2):
                cols = slice(block * quarter, (block + 1) * quarter)
                query = query_ref[rows, cols]
                grad = grad_ref[rows, cols]
                delta = jnp.sum(grad.astype(F32) * mixture_ref[rows, cols], axis=0, keepdims=True)
                log_total = total_ref[pl.ds(number, 1), cols]
                grad_query = jnp.zeros((HD, quarter), F32)
                for b, e in REACH[core][block]:
                    span = slice(b * quarter, e * quarter)
                    scores = mm(turned_key_ref[span, :], query, 1, 0) + bias_ref[span, cols]
                    probs = jnp.exp(scores - log_total)
                    grad_probs = mm(turned_value_ref[span, :], grad, 1, 0)
                    grad_scores = (probs * (grad_probs - delta)).astype(BF)
                    grad_query = grad_query + mm(key_ref[:, span], grad_scores, 1, 0)
                    grad_key_ref[:, span] += mm(query, grad_scores, 1, 1)
                    grad_value_ref[:, span] += mm(grad, probs.astype(BF), 1, 1)
                grad_query_ref[rows, cols] = grad_query
            return carry
        lax.fori_loop(0, GROUP, head, 0)

    pl.when(core_ref[0] == 0)(lambda: branch(0))
    pl.when(core_ref[0] != 0)(lambda: branch(1))

def attend_back(core, starts, query, key_values, grad_mixed, mixture, log_total):
    tokens = query.shape[1]
    spec = lambda rows, count: pl.BlockSpec((rows, count), lambda g, c: (g, 0))
    return pl.pallas_call(
        backward_kernel,
        out_shape=(jax.ShapeDtypeStruct((H * HD, tokens), F32), jax.ShapeDtypeStruct((KVH * HD, 2 * tokens), F32), jax.ShapeDtypeStruct((KVH * HD, 2 * tokens), F32)),
        grid_spec=pltpu.PrefetchScalarGridSpec(
            num_scalar_prefetch=1, grid=(KVH,),
            in_specs=[pl.BlockSpec((1, tokens), lambda g, c: (0, 0)), spec(GROUP * HD, tokens), spec(HD, 2 * tokens),
                      pl.BlockSpec((HD, 2 * tokens), lambda g, c: (g + KVH, 0)), spec(GROUP * HD, tokens), spec(GROUP * HD, tokens),
                      pl.BlockSpec((None, 8, tokens), lambda g, c: (g, 0, 0))],
            out_specs=[spec(GROUP * HD, tokens), spec(HD, 2 * tokens), spec(HD, 2 * tokens)],
            scratch_shapes=[pltpu.VMEM((2 * tokens, tokens), F32), pltpu.VMEM((2 * tokens, HD), BF), pltpu.VMEM((2 * tokens, HD), BF)],
        ),
        compiler_params=pltpu.CompilerParams(vmem_limit_bytes=40 * 2**20),
        cost_estimate=pl.CostEstimate(flops=10 * H * HD * 2 * tokens * tokens, bytes_accessed=16 * H * HD * tokens, transcendentals=H * tokens * tokens),
        name="attend_back",
    )(core, starts, query, key_values, key_values, grad_mixed, mixture, log_total)


def swap(value, axis, distance):
    count = lax.axis_size(axis)
    return lax.ppermute(value, axis, [(i, i ^ distance) for i in range(count)])


def row_slots(value):
    return [value] + [swap(value, "row", k) for k in range(1, lax.axis_size("row"))]


def dp_slots(value):
    count = lax.axis_size("dp")
    if count != 4:
        return [value] + [swap(value, "dp", k) for k in range(1, count)]
    half = value.shape[0] // 2
    near = swap(value, "dp", 1)
    far = swap(value, "dp", 2)
    both = jnp.concatenate([swap(far[:half], "dp", 1), swap(near[half:], "dp", 2)], axis=0)
    return [value, near, far, both]


def dp_direct(value):
    return [value] + [swap(value, "dp", k) for k in range(1, lax.axis_size("dp"))]


def tree_sum(values):
    while len(values) > 1:
        values = [values[i] + values[i + 1] for i in range(0, len(values), 2)]
    return values[0]


def dot(left, right, left_dim, right_dim, kind=F32):
    return lax.dot_general(
        left, right, (((left_dim,), (right_dim,)), ((), ())), preferred_element_type=F32
    ).astype(kind)


def reduce_rows(partial):
    count = lax.axis_size("row")
    size = partial.shape[0] // count
    total = partial[:size].astype(F32)
    for k in range(1, count):
        piece = partial[k * size : (k + 1) * size].astype(BF)
        total = total + swap(piece, "row", k).astype(F32)
    return total


def reduce_dp_slots(slots):
    count = len(slots)
    if count != 4:
        total = slots[0]
        for k in range(1, count):
            total = total + swap(slots[k].astype(BF), "dp", k).astype(F32)
        return total
    half = slots[0].shape[0] // 2
    top = [s[:half] for s in slots]
    low = [s[half:] for s in slots]
    got = swap(jnp.stack([top[1].astype(BF), top[3].astype(BF)]), "dp", 1)
    top_sum = top[0] + got[0].astype(F32)
    top_far = top[2] + got[1].astype(F32)
    got = swap(jnp.stack([low[2].astype(BF), low[3].astype(BF)]), "dp", 2)
    low_sum = low[0] + got[0].astype(F32)
    low_near = low[1] + got[1].astype(F32)
    top_sum = top_sum + swap(top_far.astype(BF), "dp", 2).astype(F32)
    low_sum = low_sum + swap(low_near.astype(BF), "dp", 1).astype(F32)
    return jnp.concatenate([top_sum, low_sum], axis=0)


def rms(hidden, gain):
    scale = lax.rsqrt(jnp.sum(hidden * hidden, axis=0, keepdims=True) / D + EPSILON)
    return (hidden * scale * gain).astype(BF), scale


def rms_back(grad_normed, hidden, scale, gain):
    scaled = grad_normed * gain
    inner = jnp.sum(scaled * hidden, axis=0, keepdims=True)
    grad_hidden = scale * scaled - hidden * (scale * scale * scale * inner / D)
    grad_gain = jnp.sum(grad_normed * hidden * scale, axis=1)
    return grad_hidden, grad_gain


def rotate(values, cosine, sine, heads):
    shaped = values.astype(F32).reshape(heads, 2, HD // 2, values.shape[1])
    first, second = shaped[:, 0], shaped[:, 1]
    turned = jnp.stack([first * cosine - second * sine, second * cosine + first * sine], axis=1)
    return turned.reshape(values.shape)


def chip_pairs(rows, turn):
    half = rows // 2
    pairs = []
    for r in range(rows):
        for c in range(2):
            v = r ^ turn
            pairs.append((2 * r + c, 2 * (c * half + v // 2) + v % 2))
    return pairs


def to_tokens(block, length):
    rows = lax.axis_size("row")
    me, core = lax.axis_index("row"), lax.axis_index("col")
    quarter = length // 4
    parts = []
    for v in range(rows):
        base = (v // 2) * length
        if v % 2 == 0:
            first = block[:, base : base + quarter]
            last = block[:, base + 3 * quarter : base + length]
            parts.append(jnp.concatenate([first, last], axis=1))
        else:
            parts.append(block[:, base + quarter : base + 3 * quarter])
    stacked = jnp.stack(parts)
    arrived = []
    for turn in range(rows):
        piece = lax.dynamic_index_in_dim(stacked, me ^ turn, 0, keepdims=False)
        arrived.append(lax.ppermute(piece, ("row", "col"), chip_pairs(rows, turn)))
    arrived = jnp.stack(arrived)
    origin = 2 * (me % (rows // 2)) + core
    return jnp.concatenate(
        [
            lax.dynamic_index_in_dim(arrived, me ^ k ^ origin, 0, keepdims=False)
            for k in range(rows)
        ],
        axis=0,
    )


def from_tokens(value, length):
    rows = lax.axis_size("row")
    me, core = lax.axis_index("row"), lax.axis_index("col")
    size = value.shape[0] // rows
    origin = 2 * (me % (rows // 2)) + core
    stacked = value.reshape(rows, size, value.shape[1])
    arrived = []
    for turn in range(rows):
        piece = lax.dynamic_index_in_dim(stacked, origin ^ turn ^ me, 0, keepdims=False)
        back = [(b, a) for a, b in chip_pairs(rows, turn)]
        arrived.append(lax.ppermute(piece, ("row", "col"), back))
    arrived = jnp.stack(arrived)
    quarter = length // 4
    pieces = []
    for k in range(rows // 2):
        first = lax.dynamic_index_in_dim(arrived, me ^ (2 * k), 0, keepdims=False)
        second = lax.dynamic_index_in_dim(arrived, me ^ (2 * k + 1), 0, keepdims=False)
        pieces += [first[:, :quarter], second, first[:, quarter:]]
    return jnp.concatenate(pieces, axis=1)


def own_half(tokens, core):
    quarter = tokens.shape[-1] // 4
    first = jnp.concatenate([tokens[..., :quarter], tokens[..., 3 * quarter :]], axis=-1)
    return jnp.where(core == 0, first, tokens[..., quarter : 3 * quarter])


def tie(*values):
    return lax.optimization_barrier(values)


def split_three(value):
    high = lax.reduce_precision(value, 8, 7)
    rest = value - high
    middle = lax.reduce_precision(rest, 8, 7)
    return [high.astype(BF), middle.astype(BF), (rest - middle).astype(BF)]


def shards(
    inputs,
    cotangent,
    segments,
    positions,
    attn_gain,
    w_query,
    w_key,
    w_value,
    w_out,
    ff_gain,
    w_gate,
    w_up,
    w_down,
):
    layers = w_query.shape[0]
    core = lax.axis_index("col")
    me = lax.axis_index("row")
    replica = lax.axis_index("dp")
    replicas = lax.axis_size("dp")
    rows = lax.axis_size("row")
    length = positions.shape[0]
    tokens = length // 2
    q_width = w_query.shape[2]
    k_width = w_key.shape[2]
    f_col = w_gate.shape[2]
    f_part = f_col // replicas
    at_key, at_out, at_value = q_width, q_width + k_width, 2 * q_width + k_width
    a_col = at_value + k_width
    a_part = a_col // replicas
    ff_width = 3 * f_part
    core_id = core.astype(jnp.int32)[None]

    def pack(number):
        def part(matrix):
            return lax.dynamic_slice_in_dim(matrix, replica * f_part, f_part, 1)

        return [
            w_query[number],
            w_key[number],
            w_out[number].T,
            w_value[number],
            part(w_gate[number]),
            part(w_up[number]),
            part(w_down[number].T),
        ]

    def true_rows(value):
        shaped = value.reshape(rows, -1, value.shape[-1])
        return jnp.concatenate(
            [lax.dynamic_index_in_dim(shaped, me ^ k, 0, keepdims=False) for k in range(rows)],
            axis=0,
        )

    gains = jnp.concatenate([attn_gain, ff_gain], axis=0).T
    first_pack = jnp.concatenate(pack(0) + split_three(gains), axis=1)
    later = []
    for number in range(1, layers):
        later.append(
            lax.all_gather(jnp.concatenate(pack(number), axis=1), "row", axis=0, tiled=True)
        )
    first = jnp.concatenate(row_slots(first_pack), axis=0)
    begin = a_col + ff_width
    count = 2 * layers
    gains = sum(
        first[:, begin + i * count : begin + (i + 1) * count].astype(F32) for i in range(3)
    )
    hidden = to_tokens(inputs, length).astype(F32)

    ff_slots, attn_rows = [], []
    for number in range(layers):
        block = first if number == 0 else true_rows(later[number - 1])
        attn_rows.append(block[:, :a_col])
        ff_block = block[:, a_col:begin]
        if number == 0:
            ff_slots.append(jnp.stack(dp_slots(ff_block)))
        else:
            ff_slots.append(lax.all_gather(ff_block, "dp", axis=0))

    attn_w, gu_w, down_w = [], [], []
    for number in range(layers):
        own = attn_rows[number]
        other = swap(own, "col", 1)
        attn_w.append(
            jnp.concatenate(
                [jnp.where(core == 0, own, other), jnp.where(core == 0, other, own)], axis=1
            )
        )
        near = ff_slots[number]
        far = swap(near, "col", 1)
        chunks = [near[i] for i in range(replicas)] + [far[i] for i in range(replicas)]
        gu_w.append(jnp.concatenate([c[:, : 2 * f_part] for c in chunks], axis=1))
        down_w.append(jnp.concatenate([c[:, 2 * f_part :] for c in chunks], axis=1))
    gradient_in = to_tokens(cotangent, length)

    def place_rows(query, key, out, value):
        pieces = []
        for c in range(2):
            for item, width in ((query, q_width), (key, k_width), (out, q_width), (value, k_width)):
                if item is None:
                    pieces.append(jnp.zeros((width, tokens), BF))
                else:
                    pieces.append(item[c * width : (c + 1) * width])
        return jnp.concatenate(pieces, axis=0)

    def take_rows(value, begin, width):
        return jnp.concatenate(
            [value[begin : begin + width], value[a_col + begin : a_col + begin + width]], axis=0
        )

    own_pos = own_half(positions, core)
    own_place = own_half(jnp.arange(length, dtype=jnp.int32), core)
    starts = (own_place - own_pos)[None]
    frequency = ROTARY_BASE ** (-(jnp.arange(HD // 2).astype(F32) / (HD // 2)))
    angles = frequency[:, None] * own_pos.astype(F32)[None, :]
    cosine, sine = jnp.cos(angles), jnp.sin(angles)

    kept = []
    for number in range(layers):
        gain_a = gains[:, number : number + 1]
        gain_f = gains[:, layers + number : layers + number + 1]
        normed_a, scale_a = rms(hidden, gain_a)
        qkv = dot(attn_w[number], normed_a, 0, 0, BF)
        query = rotate(take_rows(qkv, 0, q_width), cosine, sine, H)
        query = query.astype(BF) * jnp.asarray(HD**-0.5, BF)
        key = rotate(take_rows(qkv, at_key, k_width), cosine, sine, KVH).astype(BF)
        own_kv = jnp.concatenate([key, take_rows(qkv, at_value, k_width)], axis=0)
        all_kv = jnp.concatenate([own_kv, swap(own_kv, "col", 1)], axis=1)
        mixture, mixed, log_total = attend(core_id, starts, query, all_kv)
        placed = place_rows(None, None, mixed, None)
        middle = hidden + dot(attn_w[number], placed, 1, 0)
        normed_f, scale_f = rms(middle, gain_f)
        gate_up = dot(gu_w[number], normed_f, 0, 0).reshape(2 * replicas, 2, f_part, tokens)
        gate, up = gate_up[:, 0], gate_up[:, 1]
        inner = (jax.nn.silu(gate) * up).astype(BF).reshape(2 * f_col, tokens)
        kept.append(
            (hidden, scale_a, normed_a, query, all_kv, mixture, log_total, placed,
             middle, scale_f, normed_f, gate, up, inner)
        )
        hidden = middle + dot(down_w[number], inner, 1, 0)
    outputs = from_tokens(hidden.astype(BF), length)

    gradient = gradient_in.astype(F32)
    weight_grads = [None] * layers
    gain_grads = []
    pending = None
    for number in reversed(range(layers)):
        (hidden, scale_a, normed_a, query, all_kv, mixture, log_total, placed,
         middle, scale_f, normed_f, gate, up, inner) = kept[number]
        gain_a = gains[:, number : number + 1]
        gain_f = gains[:, layers + number : layers + number + 1]
        branch = gradient.astype(BF)
        grad_inner = dot(down_w[number], branch, 0, 0).reshape(gate.shape)
        sig = jax.nn.sigmoid(gate)
        grad_gate = (grad_inner * up * sig * (1.0 + gate * (1.0 - sig))).astype(BF)
        grad_up = (grad_inner * gate * sig).astype(BF)
        grad_gu = jnp.stack([grad_gate, grad_up], axis=1).reshape(4 * f_col, tokens)
        if pending is not None:
            grad_gu, pending = tie(grad_gu, pending)
            pending = lax.psum_scatter(pending, "dp", scatter_dimension=0, tiled=False)
        gu_away = dot(normed_f, grad_gu[2 * f_col :], 1, 1, BF)
        down_away = dot(branch, inner[f_col:], 1, 1, BF)
        grad_normed = dot(gu_w[number], grad_gu, 1, 0)
        grad_normed, gu_away, down_away = tie(grad_normed, gu_away, down_away)
        gu_got = swap(gu_away, "col", 1)
        down_got = swap(down_away, "col", 1)

        grad_middle, gain_f_grad = rms_back(grad_normed, middle, scale_f, gain_f)
        grad_mid = gradient + grad_middle
        branch_a = grad_mid.astype(BF)
        grad_mixed = take_rows(dot(attn_w[number], branch_a, 0, 0, BF), at_out, q_width)
        gu_sum = dot(normed_f, grad_gu[: 2 * f_col], 1, 1) + gu_got.astype(F32)
        down_sum = dot(branch, inner[:f_col], 1, 1) + down_got.astype(F32)
        slots = [
            [
                gu_sum[:, 2 * f_part * i : 2 * f_part * (i + 1)],
                down_sum[:, f_part * i : f_part * (i + 1)],
            ]
            for i in range(replicas)
        ]
        if number == 0:
            slots = [jnp.concatenate(s, axis=1) for s in slots]
            grad_mixed, *slots = tie(grad_mixed, *slots)
            ff_part = reduce_dp_slots(slots)
        grad_query, grad_keys, grad_values = attend_back(
            core_id, starts, query, all_kv, grad_mixed, mixture, log_total
        )
        grad_kv = jnp.concatenate([grad_keys, grad_values], axis=0)
        kv_got = swap(grad_kv[:, tokens:].astype(BF), "col", 1)
        grad_kv = grad_kv[:, :tokens] + kv_got.astype(F32)
        grad_query_raw = rotate(grad_query * HD**-0.5, cosine, -sine, H).astype(BF)
        grad_key_raw = rotate(grad_kv[: KVH * HD], cosine, -sine, KVH).astype(BF)
        grad_value_raw = grad_kv[KVH * HD :].astype(BF)
        grad_qkv = place_rows(grad_query_raw, grad_key_raw, None, grad_value_raw)
        grad_normed_a = dot(attn_w[number], grad_qkv, 1, 0)
        grad_lower, gain_a_grad = rms_back(grad_normed_a, hidden, scale_a, gain_a)
        gain_grads = [gain_a_grad, gain_f_grad] + gain_grads
        gradient = grad_mid + grad_lower

        def attn_dot(index, kind):
            def part(value):
                return lax.dynamic_slice_in_dim(value, index * a_col, a_col, 0)

            total = dot(normed_a, part(grad_qkv), 1, 1) + dot(branch_a, part(placed), 1, 1)
            return total.astype(kind)

        attn_away = attn_dot(1 - core, BF)
        if number > 0:
            gradient, attn_away = tie(gradient, attn_away)
            attn_sum = attn_dot(core, F32) + swap(attn_away, "col", 1).astype(F32)
            pending = jnp.stack(
                [
                    jnp.concatenate(
                        s + [attn_sum[:, a_part * i : a_part * (i + 1)]], axis=1
                    ).astype(BF)
                    for i, s in enumerate(slots)
                ]
            )
            scattered = pending
        else:
            gain_all = jnp.stack(gain_grads, axis=1)
            gain_all = split_three(gain_all)[:2]
            attn_away = jnp.concatenate([attn_away] + gain_all, axis=1)
            attn_own = jnp.concatenate(
                [attn_dot(core, F32)] + [g.astype(F32) for g in gain_all], axis=1
            )
            attn_sum = reduce_rows(attn_own + swap(attn_away, "col", 1).astype(F32))
            attn_total = tree_sum([v.astype(F32) for v in dp_direct(attn_sum.astype(BF))])
            ff_total = jnp.stack(dp_direct(reduce_rows(ff_part).astype(BF)))
    input_grad = from_tokens(gradient.astype(BF), length).astype(F32)
    last_total = lax.psum_scatter(true_rows(pending), "row", scatter_dimension=0, tiled=True)
    last_total = lax.all_gather(last_total, "dp", axis=0)

    def ff_of(number, begin, end):
        if number == 0:
            parts = [
                lax.dynamic_index_in_dim(ff_total, replica ^ i, 0, keepdims=False)
                for i in range(replicas)
            ]
        else:
            parts = [last_total[i] for i in range(replicas)]
        return jnp.concatenate([p[:, begin:end] for p in parts], axis=1).astype(F32)

    def attn_of(number, begin, end):
        if number == 0:
            return attn_total[:, begin:end]
        whole = jnp.concatenate([last_total[i][:, ff_width:] for i in range(replicas)], axis=1)
        return whole[:, begin:end].astype(F32)

    def stack(function):
        return jnp.stack([function(number) for number in range(layers)])

    gain_total = (
        attn_total[:, a_col : a_col + 2 * layers] + attn_total[:, a_col + 2 * layers :]
    ).T.reshape(layers, 2, -1)

    return (
        outputs,
        input_grad,
        gain_total[:, 0],
        stack(lambda n: attn_of(n, 0, at_key)),
        stack(lambda n: attn_of(n, at_key, at_out)),
        stack(lambda n: attn_of(n, at_value, a_col)),
        stack(lambda n: attn_of(n, at_out, at_value).T),
        gain_total[:, 1],
        stack(lambda n: ff_of(n, 0, f_part)),
        stack(lambda n: ff_of(n, f_part, 2 * f_part)),
        stack(lambda n: ff_of(n, 2 * f_part, ff_width).T),
    )


def solution(mesh):
    return jax.shard_map(
        shards,
        mesh=mesh,
        in_specs=(
            P("row", ("dp", "col")),
            P("row", ("dp", "col")),
            P(("dp", "row")),
            P(("dp", "row")),
            P(None, "row"),
            P(None, "row", "col"),
            P(None, "row", "col"),
            P(None, "row", "col"),
            P(None, "col", "row"),
            P(None, "row"),
            P(None, "row", "col"),
            P(None, "row", "col"),
            P(None, "col", "row"),
        ),
        out_specs=(
            P("row", ("dp", "col")),
            P("row", ("dp", "col")),
            P(None, "row"),
            P(None, "row", "col"),
            P(None, "row", "col"),
            P(None, "row", "col"),
            P(None, "col", "row"),
            P(None, "row"),
            P(None, "row", "col"),
            P(None, "row", "col"),
            P(None, "col", "row"),
        ),
        check_vma=False,
    )
```

```python
import functools

import jax
import jax.numpy as jnp
from jax import lax
from jax.experimental import pallas as pl
from jax.experimental.pallas import tpu as pltpu
from jax.sharding import PartitionSpec as P

D = 576
H = 9
KVH = 3
HD = 64
GROUP = H // KVH

EPSILON = 1e-05
ROTARY_BASE = 100000.0
NEGATIVE = -1e30
BF = jnp.bfloat16
F32 = jnp.float32

ORDER = ((0, 3, 1, 2), (1, 2, 0, 3))
REACH = ((((0, 1),), ((0, 4),)), (((0, 1), (2, 3)), ((0, 3),)))

def mm(left, right, left_dim, right_dim):
    return lax.dot_general(left, right, (((left_dim,), (right_dim,)), ((), ())), preferred_element_type=F32)

def fill_bias(core, start_ref, bias_ref, quarter):
    for block in range(2):
        cols = slice(block * quarter, (block + 1) * quarter)
        query_place = lax.broadcasted_iota(jnp.int32, (quarter, quarter), 1) + ORDER[core][block] * quarter
        for begin, end in REACH[core][block]:
            for part in range(begin, end):
                key_place = lax.broadcasted_iota(jnp.int32, (quarter, quarter), 0) + ORDER[core][part] * quarter
                allowed = (key_place <= query_place) & (key_place >= start_ref[:, cols])
                bias_ref[part * quarter : (part + 1) * quarter, cols] = jnp.where(allowed, 0.0, NEGATIVE)

def forward_kernel(core_ref, start_ref, query_ref, key_ref, value_ref, mixture_ref, mixed_ref, total_ref, bias_ref, turned_ref):
    quarter = query_ref.shape[1] // 2
    turned_ref[...] = key_ref[...].T

    def branch(core):
        @pl.when(pl.program_id(0) == 0)
        def _():
            fill_bias(core, start_ref, bias_ref, quarter)

        def head(number, carry):
            rows = pl.ds(number * HD, HD)
            for block in range(2):
                cols = slice(block * quarter, (block + 1) * quarter)
                query = query_ref[rows, cols]
                spans = [slice(b * quarter, e * quarter) for b, e in REACH[core][block]]
                scores = [mm(turned_ref[span, :], query, 1, 0) + bias_ref[span, cols] for span in spans]
                largest = functools.reduce(jnp.maximum, [jnp.max(s, axis=0, keepdims=True) for s in scores])
                raised = [jnp.exp(s - largest) for s in scores]
                total = sum(jnp.sum(r, axis=0, keepdims=True) for r in raised)
                mixture = sum(mm(value_ref[:, span], r.astype(BF), 1, 0) for span, r in zip(spans, raised))
                mixture = mixture / total
                mixture_ref[rows, cols] = mixture
                mixed_ref[rows, cols] = mixture.astype(BF)
                total_ref[pl.ds(number, 1), cols] = largest + jnp.log(total)
            return carry
        lax.fori_loop(0, GROUP, head, 0)

    pl.when(core_ref[0] == 0)(lambda: branch(0))
    pl.when(core_ref[0] != 0)(lambda: branch(1))

def attend(core, starts, query, key_values):
    tokens = query.shape[1]
    spec = lambda rows, count: pl.BlockSpec((rows, count), lambda g, c: (g, 0))
    return pl.pallas_call(
        forward_kernel,
        out_shape=(jax.ShapeDtypeStruct((H * HD, tokens), F32), jax.ShapeDtypeStruct((H * HD, tokens), BF), jax.ShapeDtypeStruct((KVH, 8, tokens), F32)),
        grid_spec=pltpu.PrefetchScalarGridSpec(
            num_scalar_prefetch=1, grid=(KVH,),
            in_specs=[pl.BlockSpec((1, tokens), lambda g, c: (0, 0)), spec(GROUP * HD, tokens), spec(HD, 2 * tokens),
                      pl.BlockSpec((HD, 2 * tokens), lambda g, c: (g + KVH, 0))],
            out_specs=[spec(GROUP * HD, tokens), spec(GROUP * HD, tokens), pl.BlockSpec((None, 8, tokens), lambda g, c: (g, 0, 0))],
            scratch_shapes=[pltpu.VMEM((2 * tokens, tokens), F32), pltpu.VMEM((2 * tokens, HD), BF)],
        ),
        compiler_params=pltpu.CompilerParams(vmem_limit_bytes=40 * 2**20),
        cost_estimate=pl.CostEstimate(flops=4 * H * HD * 2 * tokens * tokens, bytes_accessed=8 * H * HD * tokens, transcendentals=H * tokens * tokens),
        name="attend",
    )(core, starts, query, key_values, key_values)

def backward_kernel(core_ref, start_ref, query_ref, key_ref, value_ref, grad_ref, mixture_ref, total_ref,
                    grad_query_ref, grad_key_ref, grad_value_ref, bias_ref, turned_key_ref, turned_value_ref):
    quarter = query_ref.shape[1] // 2
    turned_key_ref[...] = key_ref[...].T
    turned_value_ref[...] = value_ref[...].T
    grad_key_ref[...] = jnp.zeros_like(grad_key_ref)
    grad_value_ref[...] = jnp.zeros_like(grad_value_ref)

    def branch(core):
        @pl.when(pl.program_id(0) == 0)
        def _():
            fill_bias(core, start_ref, bias_ref, quarter)

        def head(number, carry):
            rows = pl.ds(number * HD, HD)
            for block in range(2):
                cols = slice(block * quarter, (block + 1) * quarter)
                query = query_ref[rows, cols]
                grad = grad_ref[rows, cols]
                delta = jnp.sum(grad.astype(F32) * mixture_ref[rows, cols], axis=0, keepdims=True)
                log_total = total_ref[pl.ds(number, 1), cols]
                grad_query = jnp.zeros((HD, quarter), F32)
                for b, e in REACH[core][block]:
                    span = slice(b * quarter, e * quarter)
                    scores = mm(turned_key_ref[span, :], query, 1, 0) + bias_ref[span, cols]
                    probs = jnp.exp(scores - log_total)
                    grad_probs = mm(turned_value_ref[span, :], grad, 1, 0)
                    grad_scores = (probs * (grad_probs - delta)).astype(BF)
                    grad_query = grad_query + mm(key_ref[:, span], grad_scores, 1, 0)
                    grad_key_ref[:, span] += mm(query, grad_scores, 1, 1)
                    grad_value_ref[:, span] += mm(grad, probs.astype(BF), 1, 1)
                grad_query_ref[rows, cols] = grad_query
            return carry
        lax.fori_loop(0, GROUP, head, 0)

    pl.when(core_ref[0] == 0)(lambda: branch(0))
    pl.when(core_ref[0] != 0)(lambda: branch(1))

def attend_back(core, starts, query, key_values, grad_mixed, mixture, log_total):
    tokens = query.shape[1]
    spec = lambda rows, count: pl.BlockSpec((rows, count), lambda g, c: (g, 0))
    return pl.pallas_call(
        backward_kernel,
        out_shape=(jax.ShapeDtypeStruct((H * HD, tokens), F32), jax.ShapeDtypeStruct((KVH * HD, 2 * tokens), F32), jax.ShapeDtypeStruct((KVH * HD, 2 * tokens), F32)),
        grid_spec=pltpu.PrefetchScalarGridSpec(
            num_scalar_prefetch=1, grid=(KVH,),
            in_specs=[pl.BlockSpec((1, tokens), lambda g, c: (0, 0)), spec(GROUP * HD, tokens), spec(HD, 2 * tokens),
                      pl.BlockSpec((HD, 2 * tokens), lambda g, c: (g + KVH, 0)), spec(GROUP * HD, tokens), spec(GROUP * HD, tokens),
                      pl.BlockSpec((None, 8, tokens), lambda g, c: (g, 0, 0))],
            out_specs=[spec(GROUP * HD, tokens), spec(HD, 2 * tokens), spec(HD, 2 * tokens)],
            scratch_shapes=[pltpu.VMEM((2 * tokens, tokens), F32), pltpu.VMEM((2 * tokens, HD), BF), pltpu.VMEM((2 * tokens, HD), BF)],
        ),
        compiler_params=pltpu.CompilerParams(vmem_limit_bytes=40 * 2**20),
        cost_estimate=pl.CostEstimate(flops=10 * H * HD * 2 * tokens * tokens, bytes_accessed=16 * H * HD * tokens, transcendentals=H * tokens * tokens),
        name="attend_back",
    )(core, starts, query, key_values, key_values, grad_mixed, mixture, log_total)


def chunk_specs(near, part):
    count, width, lanes = near.shape
    return [
        pl.BlockSpec((None, width, lanes), lambda c: (jnp.minimum(c, count - 1), 0, 0)),
        pl.BlockSpec((None, width, lanes), lambda c: (jnp.maximum(c - count, 0), 0, 0)),
    ]


def ff_forward_kernel(part, count, normed_ref, middle_ref, near_ref, far_ref, hidden_ref, kept_ref):
    step = pl.program_id(0)

    @pl.when(step == 0)
    def _():
        hidden_ref[...] = middle_ref[...]

    def work(ref):
        gate_up = mm(ref[:, : 2 * part].T, normed_ref[...], 1, 0)
        kept_ref[...] = gate_up
        gate, up = gate_up[:part], gate_up[part:]
        inner = (gate * jax.nn.sigmoid(gate) * up).astype(BF)
        hidden_ref[...] += mm(ref[:, 2 * part : 3 * part], inner, 1, 0)

    pl.when(step < count)(lambda: work(near_ref))
    pl.when(step >= count)(lambda: work(far_ref))


def ff_forward(normed, middle, near, far, part):
    width, tokens = normed.shape
    count = near.shape[0]
    whole = pl.BlockSpec((width, tokens), lambda c: (0, 0))
    return pl.pallas_call(
        functools.partial(ff_forward_kernel, part, count),
        out_shape=(
            jax.ShapeDtypeStruct((width, tokens), F32),
            jax.ShapeDtypeStruct((2 * count, 2 * part, tokens), F32),
        ),
        grid=(2 * count,),
        in_specs=[whole, whole] + chunk_specs(near, part),
        out_specs=[whole, pl.BlockSpec((None, 2 * part, tokens), lambda c: (c, 0, 0))],
        compiler_params=pltpu.CompilerParams(vmem_limit_bytes=40 * 2**20),
        cost_estimate=pl.CostEstimate(
            flops=2 * 3 * width * 2 * count * part * tokens,
            bytes_accessed=20 * 2**20,
            transcendentals=2 * count * part * tokens,
        ),
        name="ff_forward",
    )(normed, middle, near, far)


def ff_backward_kernel(part, chained, order_ref, *refs):
    normed_ref, branch_ref, kept_ref, chunk_ref = refs[:4]
    total_ref, weight_ref = refs[-2:]
    step = pl.program_id(0)

    @pl.when(step == 0)
    def _():
        total_ref[...] = refs[4][...] if chained else jnp.zeros_like(total_ref)

    gate, up = kept_ref[:part], kept_ref[part:]
    grad_inner = mm(chunk_ref[:, 2 * part : 3 * part].T, branch_ref[...], 1, 0)
    sig = jax.nn.sigmoid(gate)
    silu = gate * sig
    grad_gate = (grad_inner * up * sig * (1.0 + gate * (1.0 - sig))).astype(BF)
    grad_up = (grad_inner * silu).astype(BF)
    inner = (silu * up).astype(BF)
    grad_gu = jnp.concatenate([grad_gate, grad_up], axis=0)
    total_ref[...] += mm(chunk_ref[:, : 2 * part], grad_gu, 1, 0)
    weight_ref[:, : 2 * part] = mm(normed_ref[...], grad_gu, 1, 1).astype(BF)
    weight_ref[:, 2 * part :] = mm(branch_ref[...], inner, 1, 1).astype(BF)


def ff_backward(order, normed, branch, kept, chunks, part, first, before=None):
    width, tokens = normed.shape
    count, _, lanes = chunks.shape
    whole = pl.BlockSpec((width, tokens), lambda c, order: (0, 0))
    chained = before is not None
    return pl.pallas_call(
        functools.partial(ff_backward_kernel, part, chained),
        out_shape=(
            jax.ShapeDtypeStruct((width, tokens), F32),
            jax.ShapeDtypeStruct((count, width, 3 * part), BF),
        ),
        grid_spec=pltpu.PrefetchScalarGridSpec(
            num_scalar_prefetch=1,
            grid=(count,),
            in_specs=[
                whole,
                whole,
                pl.BlockSpec((None, 2 * part, tokens), lambda c, order: (c + first, 0, 0)),
                pl.BlockSpec((None, width, lanes), lambda c, order: (c, 0, 0)),
            ]
            + ([whole] if chained else []),
            out_specs=[
                whole,
                pl.BlockSpec((None, width, 3 * part), lambda c, order: (order[c], 0, 0)),
            ],
        ),
        compiler_params=pltpu.CompilerParams(vmem_limit_bytes=40 * 2**20),
        cost_estimate=pl.CostEstimate(
            flops=2 * 6 * width * count * part * tokens,
            bytes_accessed=16 * 2**20,
            transcendentals=count * part * tokens,
        ),
        name="ff_backward",
    )(order, normed, branch, kept, chunks, *([before] if chained else []))


def swap(value, axis, distance):
    count = lax.axis_size(axis)
    return lax.ppermute(value, axis, [(i, i ^ distance) for i in range(count)])


def row_slots(value):
    return [value] + [swap(value, "row", k) for k in range(1, lax.axis_size("row"))]


def dp_step(value, turn):
    pairs = []
    for d in range(lax.axis_size("dp")):
        for c in range(2):
            distance = 1 if c == turn else 2
            pairs.append((2 * d + c, 2 * (d ^ distance) + c))
    return lax.ppermute(value, ("dp", "col"), pairs)


def place(core, slot):
    return jnp.where((core == 0) & ((slot == 1) | (slot == 2)), 3 - slot, slot)


def spread_first(value):
    return [value, swap(value, "dp", 1), swap(value, "dp", 2)]


def spread_second(parts):
    value, near, far = parts
    half = value.shape[0] // 2
    both = jnp.concatenate([swap(far[:half], "dp", 1), swap(near[half:], "dp", 2)], axis=0)
    return [value, near, far, both]


def dp_direct(value):
    return [value] + [swap(value, "dp", k) for k in range(1, lax.axis_size("dp"))]


def dp_first(value):
    return [value, dp_step(value, 1)]


def dp_second(parts):
    both = jnp.stack(parts)
    return jnp.concatenate([both, dp_step(both, 0)], axis=0)


def dp_gather(value):
    return dp_second(dp_first(value))


def reduce_dp_first(parts):
    got = dp_step(parts[2:], 0).astype(F32)
    return [(parts[1].astype(F32) + got[1]).astype(BF), parts[0].astype(F32) + got[0]]


def reduce_dp_second(parts):
    far, own = parts
    return own + dp_step(far, 1).astype(F32)


def dot(left, right, left_dim, right_dim, kind=F32):
    return lax.dot_general(
        left, right, (((left_dim,), (right_dim,)), ((), ())), preferred_element_type=F32
    ).astype(kind)


def reduce_rows(partial):
    count = lax.axis_size("row")
    size = partial.shape[0] // count
    total = partial[:size].astype(F32)
    for k in range(1, count):
        piece = partial[k * size : (k + 1) * size].astype(BF)
        total = total + swap(piece, "row", k).astype(F32)
    return total


def rms(hidden, gain):
    scale = lax.rsqrt(jnp.sum(hidden * hidden, axis=0, keepdims=True) / D + EPSILON)
    return (hidden * scale * gain).astype(BF), scale


def rms_back(grad_normed, hidden, scale, gain):
    scaled = grad_normed * gain
    inner = jnp.sum(scaled * hidden, axis=0, keepdims=True)
    grad_hidden = scale * scaled - hidden * (scale * scale * scale * inner / D)
    grad_gain = jnp.sum(grad_normed * hidden * scale, axis=1)
    return grad_hidden, grad_gain


def rotate(values, cosine, sine, heads):
    shaped = values.astype(F32).reshape(heads, 2, HD // 2, values.shape[1])
    first, second = shaped[:, 0], shaped[:, 1]
    turned = jnp.stack([first * cosine - second * sine, second * cosine + first * sine], axis=1)
    return turned.reshape(values.shape)


def chip_pairs(rows, turn):
    half = rows // 2
    pairs = []
    for r in range(rows):
        for c in range(2):
            v = r ^ turn
            pairs.append((2 * r + c, 2 * (c * half + v // 2) + v % 2))
    return pairs


def to_tokens(block, length):
    rows = lax.axis_size("row")
    me, core = lax.axis_index("row"), lax.axis_index("col")
    quarter = length // 4
    parts = []
    for v in range(rows):
        base = (v // 2) * length
        if v % 2 == 0:
            first = block[:, base : base + quarter]
            last = block[:, base + 3 * quarter : base + length]
            parts.append(jnp.concatenate([first, last], axis=1))
        else:
            parts.append(block[:, base + quarter : base + 3 * quarter])
    stacked = jnp.stack(parts)
    arrived = []
    for turn in range(rows):
        piece = lax.dynamic_index_in_dim(stacked, me ^ turn, 0, keepdims=False)
        arrived.append(lax.ppermute(piece, ("row", "col"), chip_pairs(rows, turn)))
    arrived = jnp.stack(arrived)
    origin = 2 * (me % (rows // 2)) + core
    return jnp.concatenate(
        [
            lax.dynamic_index_in_dim(arrived, me ^ k ^ origin, 0, keepdims=False)
            for k in range(rows)
        ],
        axis=0,
    )


def from_tokens(value, length):
    rows = lax.axis_size("row")
    me, core = lax.axis_index("row"), lax.axis_index("col")
    size = value.shape[0] // rows
    origin = 2 * (me % (rows // 2)) + core
    stacked = value.reshape(rows, size, value.shape[1])
    arrived = []
    for turn in range(rows):
        piece = lax.dynamic_index_in_dim(stacked, origin ^ turn ^ me, 0, keepdims=False)
        back = [(b, a) for a, b in chip_pairs(rows, turn)]
        arrived.append(lax.ppermute(piece, ("row", "col"), back))
    arrived = jnp.stack(arrived)
    quarter = length // 4
    pieces = []
    for k in range(rows // 2):
        first = lax.dynamic_index_in_dim(arrived, me ^ (2 * k), 0, keepdims=False)
        second = lax.dynamic_index_in_dim(arrived, me ^ (2 * k + 1), 0, keepdims=False)
        pieces += [first[:, :quarter], second, first[:, quarter:]]
    return jnp.concatenate(pieces, axis=1)


def own_half(tokens, core):
    quarter = tokens.shape[-1] // 4
    first = jnp.concatenate([tokens[..., :quarter], tokens[..., 3 * quarter :]], axis=-1)
    return jnp.where(core == 0, first, tokens[..., quarter : 3 * quarter])


def tie(*values):
    return lax.optimization_barrier(values)


def split_three(value):
    high = lax.reduce_precision(value, 8, 7)
    rest = value - high
    middle = lax.reduce_precision(rest, 8, 7)
    return [high.astype(BF), middle.astype(BF), (rest - middle).astype(BF)]


def shards(
    inputs,
    cotangent,
    segments,
    positions,
    attn_gain,
    w_query,
    w_key,
    w_value,
    w_out,
    ff_gain,
    w_gate,
    w_up,
    w_down,
):
    layers = w_query.shape[0]
    core = lax.axis_index("col")
    me = lax.axis_index("row")
    replica = lax.axis_index("dp")
    replicas = lax.axis_size("dp")
    rows = lax.axis_size("row")
    length = positions.shape[0]
    tokens = length // 2
    q_width = w_query.shape[2]
    k_width = w_key.shape[2]
    f_col = w_gate.shape[2]
    f_part = f_col // replicas
    at_key, at_out, at_value = q_width, q_width + k_width, 2 * q_width + k_width
    a_col = at_value + k_width
    a_part = a_col // replicas
    ff_width = 3 * f_part
    qkv_col = q_width + 2 * k_width
    core_id = core.astype(jnp.int32)[None]

    def attn_pack(number):
        whole = jnp.concatenate(
            [w_query[number], w_key[number], w_out[number].T, w_value[number]], axis=1
        )
        return lax.dynamic_slice_in_dim(whole, replica * a_part, a_part, 1)

    def ff_pack(number):
        def part(matrix):
            return lax.dynamic_slice_in_dim(matrix, replica * f_part, f_part, 1)

        return jnp.concatenate(
            [part(w_gate[number]), part(w_up[number]), part(w_down[number].T)], axis=1
        )

    def true_rows(value):
        shaped = value.reshape(rows, -1, value.shape[-1])
        return jnp.concatenate(
            [lax.dynamic_index_in_dim(shaped, me ^ k, 0, keepdims=False) for k in range(rows)],
            axis=0,
        )

    gains = jnp.concatenate([attn_gain, ff_gain], axis=0).T
    first_pack = jnp.concatenate([attn_pack(0)] + split_three(gains), axis=1)
    first = jnp.concatenate(row_slots(first_pack), axis=0)
    gains = sum(
        first[:, a_part + 2 * layers * i : a_part + 2 * layers * (i + 1)].astype(F32)
        for i in range(3)
    )
    inputs, first_pack = tie(inputs, first_pack)
    hidden = to_tokens(inputs, length).astype(F32)
    attn_near = jnp.stack(dp_direct(first[:, :a_part]))
    pack = jnp.concatenate([ff_pack(0)] + [attn_pack(n) for n in range(1, layers)], axis=1)
    pack, first = tie(pack, first)
    block = jnp.concatenate(row_slots(pack), axis=0)

    def attn_matrix(near, far):
        both = jnp.concatenate([near, far], axis=0)
        return jnp.concatenate(
            [
                lax.dynamic_index_in_dim(
                    both, (core ^ c) * replicas + (replica ^ i), 0, keepdims=False
                )
                for c in range(2)
                for i in range(replicas)
            ],
            axis=1,
        )

    def place_rows(query, key, out, value):
        pieces = []
        for c in range(2):
            for item, width in ((query, q_width), (key, k_width), (out, q_width), (value, k_width)):
                if item is None:
                    pieces.append(jnp.zeros((width, tokens), BF))
                else:
                    pieces.append(item[c * width : (c + 1) * width])
        return jnp.concatenate(pieces, axis=0)

    def take_rows(value, begin, width):
        return jnp.concatenate(
            [value[begin : begin + width], value[a_col + begin : a_col + begin + width]], axis=0
        )

    own_pos = own_half(positions, core)
    own_place = own_half(jnp.arange(length, dtype=jnp.int32), core)
    starts = (own_place - own_pos)[None]
    frequency = ROTARY_BASE ** (-(jnp.arange(HD // 2).astype(F32) / (HD // 2)))
    angles = frequency[:, None] * own_pos.astype(F32)[None, :]
    cosine, sine = jnp.cos(angles), jnp.sin(angles)

    kept = []
    attn_w, ff_w = [], []
    attn_w.append(attn_matrix(attn_near, swap(attn_near, "col", 1)))
    ff_near = spread_first(block)
    for number in range(layers):
        gain_a = gains[:, number : number + 1]
        gain_f = gains[:, layers + number : layers + number + 1]
        normed_a, scale_a = rms(hidden, gain_a)
        qkv = dot(attn_w[number], normed_a, 0, 0, BF)
        query = rotate(take_rows(qkv, 0, q_width), cosine, sine, H)
        query = query.astype(BF) * jnp.asarray(HD**-0.5, BF)
        key = rotate(take_rows(qkv, at_key, k_width), cosine, sine, KVH).astype(BF)
        own_kv = jnp.concatenate([key, take_rows(qkv, at_value, k_width)], axis=0)
        all_kv = jnp.concatenate([own_kv, swap(own_kv, "col", 1)], axis=1)
        if number + 1 < layers:
            all_kv, pack = tie(all_kv, ff_pack(number + 1))
            block = jnp.concatenate(row_slots(pack), axis=0)
        else:
            all_kv, cotangent = tie(all_kv, cotangent)
            gradient_in = to_tokens(cotangent, length)
        mixture, mixed, log_total = attend(core_id, starts, query, all_kv)
        if number == 0:
            mixed, block, *ff_near = tie(mixed, block, *ff_near)
            near = jnp.stack(spread_second(ff_near))
            ff_w.append((near, swap(near, "col", 1)))
        placed = place_rows(None, None, mixed, None)
        middle = hidden + dot(attn_w[number], placed, 1, 0)
        if number + 1 < layers:
            middle, block = tie(middle, block)
            ff_near = spread_first(block)
        normed_f, scale_f = rms(middle, gain_f)
        layer_hidden = hidden
        hidden, gate_up = ff_forward(normed_f, middle, *ff_w[number], f_part)
        kept.append(
            (layer_hidden, scale_a, normed_a, query, all_kv, mixture, log_total, placed,
             middle, scale_f, normed_f, gate_up)
        )
        if number == 0:
            near, far = ff_w[0]
            for later in range(1, layers):
                begin = ff_width + (later - 1) * a_part
                end = begin + a_part
                attn_w.append(attn_matrix(near[:, :, begin:end], far[:, :, begin:end]))
        if number + 1 < layers:
            hidden, *ff_near = tie(hidden, *ff_near)
            near = jnp.stack(spread_second(ff_near))
            ff_w.append((near, swap(near, "col", 1)))
    outputs = from_tokens(hidden.astype(BF), length)

    gradient = gradient_in.astype(F32)
    weight_grads = [None] * layers
    gain_grads = []
    pending = None
    for number in reversed(range(layers)):
        (hidden, scale_a, normed_a, query, all_kv, mixture, log_total, placed,
         middle, scale_f, normed_f, gate_up) = kept[number]
        gain_a = gains[:, number : number + 1]
        gain_f = gains[:, layers + number : layers + number + 1]
        branch = gradient.astype(BF)
        near, far = ff_w[number]
        plain = jnp.arange(replicas, dtype=jnp.int32)

        def order(c):
            return plain ^ replica if number > 0 else place(c, plain)

        grad_normed, ff_away = ff_backward(
            order(1 - core), normed_f, branch, gate_up, far, f_part, replicas
        )
        if number == 0:
            grad_normed, attn_last = tie(grad_normed, attn_last)
            attn_last = reduce_rows(attn_last).astype(BF)
        ff_got = swap(ff_away, "col", 1)
        grad_normed, ff_own = ff_backward(
            order(core), normed_f, branch, gate_up, near, f_part, 0, grad_normed
        )
        if number == 0:
            grad_normed, pending = tie(grad_normed, pending)
            pending = lax.psum_scatter(
                true_rows(pending), "row", scatter_dimension=0, tiled=True
            )

        grad_middle, gain_f_grad = rms_back(grad_normed, middle, scale_f, gain_f)
        grad_mid = gradient + grad_middle
        branch_a = grad_mid.astype(BF)
        grad_mixed = take_rows(dot(attn_w[number], branch_a, 0, 0, BF), at_out, q_width)

        def out_dot(index, kind):
            piece = lax.dynamic_slice_in_dim(placed, index * a_col + at_out, q_width, 0)
            return dot(branch_a, piece, 1, 1, kind)

        if number + 1 == layers:
            grad_mixed, outputs = tie(grad_mixed, outputs)
        ff_sum = ff_own.astype(F32) + ff_got.astype(F32)
        if number == 0:
            out_got = swap(out_dot(1 - core, BF), "col", 1)
            out_sum = out_dot(core, F32) + out_got.astype(F32)
            grad_mixed, out_sum, ff_sum = tie(grad_mixed, out_sum, ff_sum.astype(BF))
            ff_part = reduce_dp_first(ff_sum)
        else:
            grad_mixed, pending = tie(grad_mixed, ff_sum.astype(BF))
            pending = lax.psum_scatter(pending, "dp", scatter_dimension=0, tiled=False)
        grad_query, grad_keys, grad_values = attend_back(
            core_id, starts, query, all_kv, grad_mixed, mixture, log_total
        )
        if number == 0:
            grad_query, attn_last, *ff_part = tie(grad_query, attn_last, *ff_part)
            ff_part = reduce_dp_second(ff_part)
        grad_kv = jnp.concatenate([grad_keys, grad_values], axis=0)
        kv_got = swap(grad_kv[:, tokens:].astype(BF), "col", 1)
        if number == 0:
            kv_got, out_sum = tie(kv_got, out_sum)
            out_sum = reduce_rows(out_sum).astype(BF)
        grad_kv = grad_kv[:, :tokens] + kv_got.astype(F32)
        grad_query_raw = rotate(grad_query * HD**-0.5, cosine, -sine, H).astype(BF)
        grad_key_raw = rotate(grad_kv[: KVH * HD], cosine, -sine, KVH).astype(BF)
        grad_value_raw = grad_kv[KVH * HD :].astype(BF)
        grad_qkv = place_rows(grad_query_raw, grad_key_raw, None, grad_value_raw)
        grad_normed_a = dot(attn_w[number], grad_qkv, 1, 0)
        grad_lower, gain_a_grad = rms_back(grad_normed_a, hidden, scale_a, gain_a)
        gain_grads = [gain_a_grad, gain_f_grad] + gain_grads
        gradient = grad_mid + grad_lower

        def qkv_dot(index, kind):
            def part(begin, width):
                return lax.dynamic_slice_in_dim(grad_qkv, index * a_col + begin, width, 0)

            rows_of = jnp.concatenate(
                [part(0, at_out), part(at_value, k_width)], axis=0
            )
            return dot(normed_a, rows_of, 1, 1, kind)

        if number > 0:
            away = jnp.concatenate([qkv_dot(1 - core, BF), out_dot(1 - core, BF)], axis=1)
            gradient, away = tie(gradient, away)
            own = jnp.concatenate([qkv_dot(core, F32), out_dot(core, F32)], axis=1)
            attn_last = own + swap(away, "col", 1).astype(F32)
        else:
            gain_all = jnp.concatenate(
                split_three(jnp.stack(gain_grads, axis=1))[:2], axis=1
            )
            qkv_away, gain_all, gradient = tie(qkv_dot(1 - core, BF), gain_all, gradient)
            qkv_got = swap(jnp.concatenate([qkv_away, gain_all], axis=1), "col", 1)
            early = jnp.concatenate([pending, attn_last, out_sum], axis=1)
            qkv_own = jnp.concatenate([qkv_dot(core, F32), gain_all.astype(F32)], axis=1)
            qkv_sum = reduce_rows(qkv_own + qkv_got.astype(F32))
            ff_total = reduce_rows(ff_part).astype(BF)
            ff_total, gradient, *early = tie(ff_total, gradient, *dp_first(early))
            ff_total = dp_gather(ff_total)
            early = dp_second(early)
            first_total = dp_gather(qkv_sum.astype(BF))
            last_total, middle_total = early[:, :, :ff_width], early[:, :, ff_width:]
    input_grad = from_tokens(gradient.astype(BF), length).astype(F32)

    def in_order(parts):
        return [
            lax.dynamic_index_in_dim(parts, place(core, replica ^ i), 0, keepdims=False)
            for i in range(replicas)
        ]

    ff_totals = [in_order(ff_total), in_order(last_total)]

    def ff_of(number, begin, end):
        return jnp.concatenate([p[:, begin:end] for p in ff_totals[number]], axis=1).astype(F32)

    def total_of(parts):
        parts = parts.astype(F32)
        return (parts[0] + parts[3]) + (parts[1] + parts[2])

    first_total, middle_total = total_of(first_total), total_of(middle_total)
    attn_whole = [
        jnp.concatenate([first_total[:, :qkv_col], middle_total[:, a_col:]], axis=1),
        middle_total[:, :a_col],
    ]

    def attn_of(number, begin, end):
        return attn_whole[number][:, begin:end]

    def stack(function):
        return jnp.stack([function(number) for number in range(layers)])

    gain_total = first_total[:, qkv_col:]
    gain_total = gain_total[:, : 2 * layers] + gain_total[:, 2 * layers :]
    gain_total = gain_total.T.reshape(layers, 2, -1)

    return (
        outputs,
        input_grad,
        gain_total[:, 0],
        stack(lambda n: attn_of(n, 0, q_width)),
        stack(lambda n: attn_of(n, q_width, q_width + k_width)),
        stack(lambda n: attn_of(n, q_width + k_width, qkv_col)),
        stack(lambda n: attn_of(n, qkv_col, a_col).T),
        gain_total[:, 1],
        stack(lambda n: ff_of(n, 0, f_part)),
        stack(lambda n: ff_of(n, f_part, 2 * f_part)),
        stack(lambda n: ff_of(n, 2 * f_part, ff_width).T),
    )


def solution(mesh):
    return jax.shard_map(
        shards,
        mesh=mesh,
        in_specs=(
            P("row", ("dp", "col")),
            P("row", ("dp", "col")),
            P(("dp", "row")),
            P(("dp", "row")),
            P(None, "row"),
            P(None, "row", "col"),
            P(None, "row", "col"),
            P(None, "row", "col"),
            P(None, "col", "row"),
            P(None, "row"),
            P(None, "row", "col"),
            P(None, "row", "col"),
            P(None, "col", "row"),
        ),
        out_specs=(
            P("row", ("dp", "col")),
            P("row", ("dp", "col")),
            P(None, "row"),
            P(None, "row", "col"),
            P(None, "row", "col"),
            P(None, "row", "col"),
            P(None, "col", "row"),
            P(None, "row"),
            P(None, "row", "col"),
            P(None, "row", "col"),
            P(None, "col", "row"),
        ),
        check_vma=False,
    )
```

```python
import functools

import jax
import jax.numpy as jnp
from jax import lax
from jax.experimental import pallas as pl
from jax.experimental.pallas import tpu as pltpu
from jax.sharding import PartitionSpec as P

D = 576
H = 9
KVH = 3
HD = 64
GROUP = H // KVH

EPSILON = 1e-05
ROTARY_BASE = 100000.0
NEGATIVE = -1e30
BF = jnp.bfloat16
F32 = jnp.float32

ORDER = ((0, 3, 1, 2), (1, 2, 0, 3))
REACH = ((((0, 1),), ((0, 4),)), (((0, 1), (2, 3)), ((0, 3),)))

def mm(left, right, left_dim, right_dim):
    return lax.dot_general(left, right, (((left_dim,), (right_dim,)), ((), ())), preferred_element_type=F32)

def fill_bias(core, start_ref, bias_ref, quarter):
    for block in range(2):
        cols = slice(block * quarter, (block + 1) * quarter)
        query_place = lax.broadcasted_iota(jnp.int32, (quarter, quarter), 1) + ORDER[core][block] * quarter
        for begin, end in REACH[core][block]:
            for part in range(begin, end):
                key_place = lax.broadcasted_iota(jnp.int32, (quarter, quarter), 0) + ORDER[core][part] * quarter
                allowed = (key_place <= query_place) & (key_place >= start_ref[:, cols])
                bias_ref[part * quarter : (part + 1) * quarter, cols] = jnp.where(allowed, 0.0, NEGATIVE)

def forward_kernel(core_ref, start_ref, query_ref, key_ref, value_ref, mixture_ref, mixed_ref, total_ref, bias_ref, turned_ref):
    quarter = query_ref.shape[1] // 2
    turned_ref[...] = key_ref[...].T

    def branch(core):
        @pl.when(pl.program_id(0) == 0)
        def _():
            fill_bias(core, start_ref, bias_ref, quarter)

        def head(number, carry):
            rows = pl.ds(number * HD, HD)
            for block in range(2):
                cols = slice(block * quarter, (block + 1) * quarter)
                query = query_ref[rows, cols]
                spans = [slice(b * quarter, e * quarter) for b, e in REACH[core][block]]
                scores = [mm(turned_ref[span, :], query, 1, 0) + bias_ref[span, cols] for span in spans]
                largest = functools.reduce(jnp.maximum, [jnp.max(s, axis=0, keepdims=True) for s in scores])
                raised = [jnp.exp(s - largest) for s in scores]
                total = sum(jnp.sum(r, axis=0, keepdims=True) for r in raised)
                mixture = sum(mm(value_ref[:, span], r.astype(BF), 1, 0) for span, r in zip(spans, raised))
                mixture = mixture / total
                mixture_ref[rows, cols] = mixture
                mixed_ref[rows, cols] = mixture.astype(BF)
                total_ref[pl.ds(number, 1), cols] = largest + jnp.log(total)
            return carry
        lax.fori_loop(0, GROUP, head, 0)

    pl.when(core_ref[0] == 0)(lambda: branch(0))
    pl.when(core_ref[0] != 0)(lambda: branch(1))

def attend(core, starts, query, key_values):
    tokens = query.shape[1]
    spec = lambda rows, count: pl.BlockSpec((rows, count), lambda g, c: (g, 0))
    return pl.pallas_call(
        forward_kernel,
        out_shape=(jax.ShapeDtypeStruct((H * HD, tokens), F32), jax.ShapeDtypeStruct((H * HD, tokens), BF), jax.ShapeDtypeStruct((KVH, 8, tokens), F32)),
        grid_spec=pltpu.PrefetchScalarGridSpec(
            num_scalar_prefetch=1, grid=(KVH,),
            in_specs=[pl.BlockSpec((1, tokens), lambda g, c: (0, 0)), spec(GROUP * HD, tokens), spec(HD, 2 * tokens),
                      pl.BlockSpec((HD, 2 * tokens), lambda g, c: (g + KVH, 0))],
            out_specs=[spec(GROUP * HD, tokens), spec(GROUP * HD, tokens), pl.BlockSpec((None, 8, tokens), lambda g, c: (g, 0, 0))],
            scratch_shapes=[pltpu.VMEM((2 * tokens, tokens), F32), pltpu.VMEM((2 * tokens, HD), BF)],
        ),
        compiler_params=pltpu.CompilerParams(vmem_limit_bytes=40 * 2**20),
        cost_estimate=pl.CostEstimate(flops=4 * H * HD * 2 * tokens * tokens, bytes_accessed=8 * H * HD * tokens, transcendentals=H * tokens * tokens),
        name="attend",
    )(core, starts, query, key_values, key_values)

def backward_kernel(core_ref, start_ref, query_ref, key_ref, value_ref, grad_ref, mixture_ref, total_ref,
                    grad_query_ref, grad_key_ref, grad_value_ref, bias_ref, turned_key_ref, turned_value_ref):
    quarter = query_ref.shape[1] // 2
    turned_key_ref[...] = key_ref[...].T
    turned_value_ref[...] = value_ref[...].T
    grad_key_ref[...] = jnp.zeros_like(grad_key_ref)
    grad_value_ref[...] = jnp.zeros_like(grad_value_ref)

    def branch(core):
        @pl.when(pl.program_id(0) == 0)
        def _():
            fill_bias(core, start_ref, bias_ref, quarter)

        def head(number, carry):
            rows = pl.ds(number * HD, HD)
            for block in range(2):
                cols = slice(block * quarter, (block + 1) * quarter)
                query = query_ref[rows, cols]
                grad = grad_ref[rows, cols]
                delta = jnp.sum(grad.astype(F32) * mixture_ref[rows, cols], axis=0, keepdims=True)
                log_total = total_ref[pl.ds(number, 1), cols]
                grad_query = jnp.zeros((HD, quarter), F32)
                for b, e in REACH[core][block]:
                    span = slice(b * quarter, e * quarter)
                    scores = mm(turned_key_ref[span, :], query, 1, 0) + bias_ref[span, cols]
                    probs = jnp.exp(scores - log_total)
                    grad_probs = mm(turned_value_ref[span, :], grad, 1, 0)
                    grad_scores = (probs * (grad_probs - delta)).astype(BF)
                    grad_query = grad_query + mm(key_ref[:, span], grad_scores, 1, 0)
                    grad_key_ref[:, span] += mm(query, grad_scores, 1, 1)
                    grad_value_ref[:, span] += mm(grad, probs.astype(BF), 1, 1)
                grad_query_ref[rows, cols] = grad_query
            return carry
        lax.fori_loop(0, GROUP, head, 0)

    pl.when(core_ref[0] == 0)(lambda: branch(0))
    pl.when(core_ref[0] != 0)(lambda: branch(1))

def attend_back(core, starts, query, key_values, grad_mixed, mixture, log_total):
    tokens = query.shape[1]
    spec = lambda rows, count: pl.BlockSpec((rows, count), lambda g, c: (g, 0))
    return pl.pallas_call(
        backward_kernel,
        out_shape=(jax.ShapeDtypeStruct((H * HD, tokens), F32), jax.ShapeDtypeStruct((KVH * HD, 2 * tokens), F32), jax.ShapeDtypeStruct((KVH * HD, 2 * tokens), F32)),
        grid_spec=pltpu.PrefetchScalarGridSpec(
            num_scalar_prefetch=1, grid=(KVH,),
            in_specs=[pl.BlockSpec((1, tokens), lambda g, c: (0, 0)), spec(GROUP * HD, tokens), spec(HD, 2 * tokens),
                      pl.BlockSpec((HD, 2 * tokens), lambda g, c: (g + KVH, 0)), spec(GROUP * HD, tokens), spec(GROUP * HD, tokens),
                      pl.BlockSpec((None, 8, tokens), lambda g, c: (g, 0, 0))],
            out_specs=[spec(GROUP * HD, tokens), spec(HD, 2 * tokens), spec(HD, 2 * tokens)],
            scratch_shapes=[pltpu.VMEM((2 * tokens, tokens), F32), pltpu.VMEM((2 * tokens, HD), BF), pltpu.VMEM((2 * tokens, HD), BF)],
        ),
        compiler_params=pltpu.CompilerParams(vmem_limit_bytes=40 * 2**20),
        cost_estimate=pl.CostEstimate(flops=10 * H * HD * 2 * tokens * tokens, bytes_accessed=16 * H * HD * tokens, transcendentals=H * tokens * tokens),
        name="attend_back",
    )(core, starts, query, key_values, key_values, grad_mixed, mixture, log_total)


def chunk_specs(near, part):
    count, width, lanes = near.shape
    return [
        pl.BlockSpec((None, width, lanes), lambda c: (jnp.minimum(c, count - 1), 0, 0)),
        pl.BlockSpec((None, width, lanes), lambda c: (jnp.maximum(c - count, 0), 0, 0)),
    ]


def ff_forward_kernel(part, count, normed_ref, middle_ref, near_ref, far_ref, hidden_ref, kept_ref):
    step = pl.program_id(0)

    @pl.when(step == 0)
    def _():
        hidden_ref[...] = middle_ref[...]

    def work(ref):
        gate_up = mm(ref[:, : 2 * part].T, normed_ref[...], 1, 0)
        kept_ref[...] = gate_up
        gate, up = gate_up[:part], gate_up[part:]
        inner = (gate * jax.nn.sigmoid(gate) * up).astype(BF)
        hidden_ref[...] += mm(ref[:, 2 * part : 3 * part], inner, 1, 0)

    pl.when(step < count)(lambda: work(near_ref))
    pl.when(step >= count)(lambda: work(far_ref))


def ff_forward(normed, middle, near, far, part):
    width, tokens = normed.shape
    count = near.shape[0]
    whole = pl.BlockSpec((width, tokens), lambda c: (0, 0))
    return pl.pallas_call(
        functools.partial(ff_forward_kernel, part, count),
        out_shape=(
            jax.ShapeDtypeStruct((width, tokens), F32),
            jax.ShapeDtypeStruct((2 * count, 2 * part, tokens), F32),
        ),
        grid=(2 * count,),
        in_specs=[whole, whole] + chunk_specs(near, part),
        out_specs=[whole, pl.BlockSpec((None, 2 * part, tokens), lambda c: (c, 0, 0))],
        compiler_params=pltpu.CompilerParams(vmem_limit_bytes=40 * 2**20),
        cost_estimate=pl.CostEstimate(
            flops=2 * 3 * width * 2 * count * part * tokens,
            bytes_accessed=20 * 2**20,
            transcendentals=2 * count * part * tokens,
        ),
        name="ff_forward",
    )(normed, middle, near, far)


def ff_backward_kernel(part, chained, order_ref, *refs):
    normed_ref, branch_ref, kept_ref, chunk_ref = refs[:4]
    total_ref, weight_ref = refs[-2:]
    step = pl.program_id(0)

    @pl.when(step == 0)
    def _():
        total_ref[...] = refs[4][...] if chained else jnp.zeros_like(total_ref)

    gate, up = kept_ref[:part], kept_ref[part:]
    grad_inner = mm(chunk_ref[:, 2 * part : 3 * part].T, branch_ref[...], 1, 0)
    sig = jax.nn.sigmoid(gate)
    silu = gate * sig
    grad_gate = (grad_inner * up * sig * (1.0 + gate * (1.0 - sig))).astype(BF)
    grad_up = (grad_inner * silu).astype(BF)
    inner = (silu * up).astype(BF)
    grad_gu = jnp.concatenate([grad_gate, grad_up], axis=0)
    total_ref[...] += mm(chunk_ref[:, : 2 * part], grad_gu, 1, 0)
    weight_ref[:, : 2 * part] = mm(normed_ref[...], grad_gu, 1, 1).astype(BF)
    weight_ref[:, 2 * part :] = mm(branch_ref[...], inner, 1, 1).astype(BF)


def ff_backward(order, normed, branch, kept, chunks, part, first, before=None):
    width, tokens = normed.shape
    count, _, lanes = chunks.shape
    whole = pl.BlockSpec((width, tokens), lambda c, order: (0, 0))
    chained = before is not None
    return pl.pallas_call(
        functools.partial(ff_backward_kernel, part, chained),
        out_shape=(
            jax.ShapeDtypeStruct((width, tokens), F32),
            jax.ShapeDtypeStruct((count, width, 3 * part), BF),
        ),
        grid_spec=pltpu.PrefetchScalarGridSpec(
            num_scalar_prefetch=1,
            grid=(count,),
            in_specs=[
                whole,
                whole,
                pl.BlockSpec((None, 2 * part, tokens), lambda c, order: (c + first, 0, 0)),
                pl.BlockSpec((None, width, lanes), lambda c, order: (c, 0, 0)),
            ]
            + ([whole] if chained else []),
            out_specs=[
                whole,
                pl.BlockSpec((None, width, 3 * part), lambda c, order: (order[c], 0, 0)),
            ],
        ),
        compiler_params=pltpu.CompilerParams(vmem_limit_bytes=40 * 2**20),
        cost_estimate=pl.CostEstimate(
            flops=2 * 6 * width * count * part * tokens,
            bytes_accessed=16 * 2**20,
            transcendentals=count * part * tokens,
        ),
        name="ff_backward",
    )(order, normed, branch, kept, chunks, *([before] if chained else []))


def swap(value, axis, distance):
    count = lax.axis_size(axis)
    return lax.ppermute(value, axis, [(i, i ^ distance) for i in range(count)])


def row_slots(value):
    return [value] + [swap(value, "row", k) for k in range(1, lax.axis_size("row"))]


def dp_step(value, turn):
    pairs = []
    for d in range(lax.axis_size("dp")):
        for c in range(2):
            distance = 1 if c == turn else 2
            pairs.append((2 * d + c, 2 * (d ^ distance) + c))
    return lax.ppermute(value, ("dp", "col"), pairs)


def place(core, slot):
    return jnp.where((core == 0) & ((slot == 1) | (slot == 2)), 3 - slot, slot)


def spread_first(value):
    return [value, swap(value, "dp", 1), swap(value, "dp", 2)]


def spread_second(parts):
    value, near, far = parts
    half = value.shape[0] // 2
    both = jnp.concatenate([swap(far[:half], "dp", 1), swap(near[half:], "dp", 2)], axis=0)
    return [value, near, far, both]


def dp_direct(value):
    return [value] + [swap(value, "dp", k) for k in range(1, lax.axis_size("dp"))]


def dp_first(value):
    return [value, dp_step(value, 1)]


def dp_second(parts):
    both = jnp.stack(parts)
    return jnp.concatenate([both, dp_step(both, 0)], axis=0)


def dp_gather(value):
    return dp_second(dp_first(value))


def reduce_dp_first(parts):
    got = dp_step(parts[2:], 0).astype(F32)
    return [(parts[1].astype(F32) + got[1]).astype(BF), parts[0].astype(F32) + got[0]]


def reduce_dp_second(parts):
    far, own = parts
    return own + dp_step(far, 1).astype(F32)


def dot(left, right, left_dim, right_dim, kind=F32):
    return lax.dot_general(
        left, right, (((left_dim,), (right_dim,)), ((), ())), preferred_element_type=F32
    ).astype(kind)


def reduce_rows(partial):
    count = lax.axis_size("row")
    size = partial.shape[0] // count
    total = partial[:size].astype(F32)
    for k in range(1, count):
        piece = partial[k * size : (k + 1) * size].astype(BF)
        total = total + swap(piece, "row", k).astype(F32)
    return total


def rms(hidden, gain):
    scale = lax.rsqrt(jnp.sum(hidden * hidden, axis=0, keepdims=True) / D + EPSILON)
    return (hidden * scale * gain).astype(BF), scale


def rms_back(grad_normed, hidden, scale, gain):
    scaled = grad_normed * gain
    inner = jnp.sum(scaled * hidden, axis=0, keepdims=True)
    grad_hidden = scale * scaled - hidden * (scale * scale * scale * inner / D)
    grad_gain = jnp.sum(grad_normed * hidden * scale, axis=1)
    return grad_hidden, grad_gain


def rotate(values, cosine, sine, heads):
    shaped = values.astype(F32).reshape(heads, 2, HD // 2, values.shape[1])
    first, second = shaped[:, 0], shaped[:, 1]
    turned = jnp.stack([first * cosine - second * sine, second * cosine + first * sine], axis=1)
    return turned.reshape(values.shape)


def chip_pairs(rows, turn):
    half = rows // 2
    pairs = []
    for r in range(rows):
        for c in range(2):
            v = r ^ turn
            pairs.append((2 * r + c, 2 * (c * half + v // 2) + v % 2))
    return pairs


def to_tokens(block, length):
    rows = lax.axis_size("row")
    me, core = lax.axis_index("row"), lax.axis_index("col")
    quarter = length // 4
    parts = []
    for v in range(rows):
        base = (v // 2) * length
        if v % 2 == 0:
            first = block[:, base : base + quarter]
            last = block[:, base + 3 * quarter : base + length]
            parts.append(jnp.concatenate([first, last], axis=1))
        else:
            parts.append(block[:, base + quarter : base + 3 * quarter])
    stacked = jnp.stack(parts)
    arrived = []
    for turn in range(rows):
        piece = lax.dynamic_index_in_dim(stacked, me ^ turn, 0, keepdims=False)
        arrived.append(lax.ppermute(piece, ("row", "col"), chip_pairs(rows, turn)))
    arrived = jnp.stack(arrived)
    origin = 2 * (me % (rows // 2)) + core
    return jnp.concatenate(
        [
            lax.dynamic_index_in_dim(arrived, me ^ k ^ origin, 0, keepdims=False)
            for k in range(rows)
        ],
        axis=0,
    )


def from_tokens(value, length):
    rows = lax.axis_size("row")
    me, core = lax.axis_index("row"), lax.axis_index("col")
    size = value.shape[0] // rows
    origin = 2 * (me % (rows // 2)) + core
    stacked = value.reshape(rows, size, value.shape[1])
    arrived = []
    for turn in range(rows):
        piece = lax.dynamic_index_in_dim(stacked, origin ^ turn ^ me, 0, keepdims=False)
        back = [(b, a) for a, b in chip_pairs(rows, turn)]
        arrived.append(lax.ppermute(piece, ("row", "col"), back))
    arrived = jnp.stack(arrived)
    quarter = length // 4
    pieces = []
    for k in range(rows // 2):
        first = lax.dynamic_index_in_dim(arrived, me ^ (2 * k), 0, keepdims=False)
        second = lax.dynamic_index_in_dim(arrived, me ^ (2 * k + 1), 0, keepdims=False)
        pieces += [first[:, :quarter], second, first[:, quarter:]]
    return jnp.concatenate(pieces, axis=1)


def own_half(tokens, core):
    quarter = tokens.shape[-1] // 4
    first = jnp.concatenate([tokens[..., :quarter], tokens[..., 3 * quarter :]], axis=-1)
    return jnp.where(core == 0, first, tokens[..., quarter : 3 * quarter])


def tie(*values):
    return lax.optimization_barrier(values)


def split_three(value):
    high = lax.reduce_precision(value, 8, 7)
    rest = value - high
    middle = lax.reduce_precision(rest, 8, 7)
    return [high.astype(BF), middle.astype(BF), (rest - middle).astype(BF)]


def shards(
    inputs,
    cotangent,
    segments,
    positions,
    attn_gain,
    w_query,
    w_key,
    w_value,
    w_out,
    ff_gain,
    w_gate,
    w_up,
    w_down,
):
    layers = w_query.shape[0]
    core = lax.axis_index("col")
    me = lax.axis_index("row")
    replica = lax.axis_index("dp")
    replicas = lax.axis_size("dp")
    rows = lax.axis_size("row")
    length = positions.shape[0]
    tokens = length // 2
    q_width = w_query.shape[2]
    k_width = w_key.shape[2]
    f_col = w_gate.shape[2]
    f_part = f_col // replicas
    at_key, at_out, at_value = q_width, q_width + k_width, 2 * q_width + k_width
    a_col = at_value + k_width
    a_part = a_col // replicas
    ff_width = 3 * f_part
    qkv_col = q_width + 2 * k_width
    core_id = core.astype(jnp.int32)[None]

    def attn_pack(number):
        whole = jnp.concatenate(
            [w_query[number], w_key[number], w_out[number].T, w_value[number]], axis=1
        )
        return lax.dynamic_slice_in_dim(whole, replica * a_part, a_part, 1)

    def ff_pack(number):
        def part(matrix):
            return lax.dynamic_slice_in_dim(matrix, replica * f_part, f_part, 1)

        return jnp.concatenate(
            [part(w_gate[number]), part(w_up[number]), part(w_down[number].T)], axis=1
        )

    def true_rows(value):
        shaped = value.reshape(rows, -1, value.shape[-1])
        return jnp.concatenate(
            [lax.dynamic_index_in_dim(shaped, me ^ k, 0, keepdims=False) for k in range(rows)],
            axis=0,
        )

    gains = jnp.concatenate([attn_gain, ff_gain], axis=0).T
    first_pack = jnp.concatenate([attn_pack(0)] + split_three(gains), axis=1)
    first = jnp.concatenate(row_slots(first_pack), axis=0)
    gains = sum(
        first[:, a_part + 2 * layers * i : a_part + 2 * layers * (i + 1)].astype(F32)
        for i in range(3)
    )
    inputs, first_pack = tie(inputs, first_pack)
    hidden = to_tokens(inputs, length).astype(F32)
    attn_near = jnp.stack(dp_direct(first[:, :a_part]))
    pack = jnp.concatenate([ff_pack(0)] + [attn_pack(n) for n in range(1, layers)], axis=1)
    pack, first = tie(pack, first)
    block = jnp.concatenate(row_slots(pack), axis=0)

    def attn_matrix(near, far):
        both = jnp.concatenate([near, far], axis=0)
        return jnp.concatenate(
            [
                lax.dynamic_index_in_dim(
                    both, (core ^ c) * replicas + (replica ^ i), 0, keepdims=False
                )
                for c in range(2)
                for i in range(replicas)
            ],
            axis=1,
        )

    def place_rows(query, key, out, value):
        pieces = []
        for c in range(2):
            for item, width in ((query, q_width), (key, k_width), (out, q_width), (value, k_width)):
                if item is None:
                    pieces.append(jnp.zeros((width, tokens), BF))
                else:
                    pieces.append(item[c * width : (c + 1) * width])
        return jnp.concatenate(pieces, axis=0)

    def take_rows(value, begin, width):
        return jnp.concatenate(
            [value[begin : begin + width], value[a_col + begin : a_col + begin + width]], axis=0
        )

    own_pos = own_half(positions, core)
    own_place = own_half(jnp.arange(length, dtype=jnp.int32), core)
    starts = (own_place - own_pos)[None]
    frequency = ROTARY_BASE ** (-(jnp.arange(HD // 2).astype(F32) / (HD // 2)))
    angles = frequency[:, None] * own_pos.astype(F32)[None, :]
    cosine, sine = jnp.cos(angles), jnp.sin(angles)

    kept = []
    attn_w, ff_w = [], []
    attn_w.append(attn_matrix(attn_near, swap(attn_near, "col", 1)))
    ff_near = spread_first(block)
    for number in range(layers):
        gain_a = gains[:, number : number + 1]
        gain_f = gains[:, layers + number : layers + number + 1]
        normed_a, scale_a = rms(hidden, gain_a)
        qkv = dot(attn_w[number], normed_a, 0, 0, BF)
        query = rotate(take_rows(qkv, 0, q_width), cosine, sine, H)
        query = query.astype(BF) * jnp.asarray(HD**-0.5, BF)
        key = rotate(take_rows(qkv, at_key, k_width), cosine, sine, KVH).astype(BF)
        own_kv = jnp.concatenate([key, take_rows(qkv, at_value, k_width)], axis=0)
        all_kv = jnp.concatenate([own_kv, swap(own_kv, "col", 1)], axis=1)
        if number + 1 < layers:
            all_kv, pack = tie(all_kv, ff_pack(number + 1))
            block = jnp.concatenate(row_slots(pack), axis=0)
        else:
            all_kv, cotangent = tie(all_kv, cotangent)
            gradient_in = to_tokens(cotangent, length)
        mixture, mixed, log_total = attend(core_id, starts, query, all_kv)
        if number == 0:
            mixed, block, *ff_near = tie(mixed, block, *ff_near)
            near = jnp.stack(spread_second(ff_near))
            ff_w.append((near, swap(near, "col", 1)))
        placed = place_rows(None, None, mixed, None)
        middle = hidden + dot(attn_w[number], placed, 1, 0)
        if number + 1 < layers:
            middle, block = tie(middle, block)
            ff_near = spread_first(block)
        normed_f, scale_f = rms(middle, gain_f)
        layer_hidden = hidden
        hidden, gate_up = ff_forward(normed_f, middle, *ff_w[number], f_part)
        kept.append(
            (layer_hidden, scale_a, normed_a, query, all_kv, mixture, log_total, placed,
             middle, scale_f, normed_f, gate_up)
        )
        if number == 0:
            near, far = ff_w[0]
            for later in range(1, layers):
                begin = ff_width + (later - 1) * a_part
                end = begin + a_part
                attn_w.append(attn_matrix(near[:, :, begin:end], far[:, :, begin:end]))
        if number + 1 < layers:
            hidden, *ff_near = tie(hidden, *ff_near)
            near = jnp.stack(spread_second(ff_near))
            ff_w.append((near, swap(near, "col", 1)))
    outputs = from_tokens(hidden.astype(BF), length)

    gradient = gradient_in.astype(F32)
    weight_grads = [None] * layers
    gain_grads = []
    pending = None
    for number in reversed(range(layers)):
        (hidden, scale_a, normed_a, query, all_kv, mixture, log_total, placed,
         middle, scale_f, normed_f, gate_up) = kept[number]
        gain_a = gains[:, number : number + 1]
        gain_f = gains[:, layers + number : layers + number + 1]
        branch = gradient.astype(BF)
        near, far = ff_w[number]
        plain = jnp.arange(replicas, dtype=jnp.int32)

        def order(c):
            return plain ^ replica if number > 0 else place(c, plain)

        grad_normed, ff_away = ff_backward(
            order(1 - core), normed_f, branch, gate_up, far, f_part, replicas
        )
        if number == 0:
            grad_normed, attn_last = tie(grad_normed, attn_last)
            attn_last = reduce_rows(attn_last).astype(BF)
        ff_got = swap(ff_away, "col", 1)
        grad_normed, ff_own = ff_backward(
            order(core), normed_f, branch, gate_up, near, f_part, 0, grad_normed
        )
        if number == 0:
            grad_normed, pending = tie(grad_normed, pending)
            pending = lax.psum_scatter(
                true_rows(pending), "row", scatter_dimension=0, tiled=True
            )

        grad_middle, gain_f_grad = rms_back(grad_normed, middle, scale_f, gain_f)
        grad_mid = gradient + grad_middle
        branch_a = grad_mid.astype(BF)
        grad_mixed = take_rows(dot(attn_w[number], branch_a, 0, 0, BF), at_out, q_width)

        def out_dot(index, kind):
            piece = lax.dynamic_slice_in_dim(placed, index * a_col + at_out, q_width, 0)
            return dot(branch_a, piece, 1, 1, kind)

        if number + 1 == layers:
            grad_mixed, outputs = tie(grad_mixed, outputs)
        ff_sum = ff_own.astype(F32) + ff_got.astype(F32)
        if number == 0:
            out_got = swap(out_dot(1 - core, BF), "col", 1)
            out_sum = out_dot(core, F32) + out_got.astype(F32)
            grad_mixed, out_sum, ff_sum = tie(grad_mixed, out_sum, ff_sum.astype(BF))
            ff_part = reduce_dp_first(ff_sum)
        else:
            grad_mixed, pending = tie(grad_mixed, ff_sum.astype(BF))
            pending = lax.psum_scatter(pending, "dp", scatter_dimension=0, tiled=False)
        grad_query, grad_keys, grad_values = attend_back(
            core_id, starts, query, all_kv, grad_mixed, mixture, log_total
        )
        if number == 0:
            grad_query, attn_last, *ff_part = tie(grad_query, attn_last, *ff_part)
            ff_part = reduce_dp_second(ff_part)
        grad_kv = jnp.concatenate([grad_keys, grad_values], axis=0)
        kv_got = swap(grad_kv[:, tokens:].astype(BF), "col", 1)
        grad_kv = grad_kv[:, :tokens] + kv_got.astype(F32)
        grad_query_raw = rotate(grad_query * HD**-0.5, cosine, -sine, H).astype(BF)
        grad_key_raw = rotate(grad_kv[: KVH * HD], cosine, -sine, KVH).astype(BF)
        grad_value_raw = grad_kv[KVH * HD :].astype(BF)
        grad_qkv = place_rows(grad_query_raw, grad_key_raw, None, grad_value_raw)
        grad_normed_a = dot(attn_w[number], grad_qkv, 1, 0)
        grad_lower, gain_a_grad = rms_back(grad_normed_a, hidden, scale_a, gain_a)
        gain_grads = [gain_a_grad, gain_f_grad] + gain_grads
        gradient = grad_mid + grad_lower

        def qkv_dot(index, kind):
            def part(begin, width):
                return lax.dynamic_slice_in_dim(grad_qkv, index * a_col + begin, width, 0)

            rows_of = jnp.concatenate(
                [part(0, at_out), part(at_value, k_width)], axis=0
            )
            return dot(normed_a, rows_of, 1, 1, kind)

        if number > 0:
            away = jnp.concatenate([qkv_dot(1 - core, BF), out_dot(1 - core, BF)], axis=1)
            gradient, away = tie(gradient, away)
            own = jnp.concatenate([qkv_dot(core, F32), out_dot(core, F32)], axis=1)
            attn_last = own + swap(away, "col", 1).astype(F32)
        else:
            gain_all = jnp.concatenate(
                split_three(jnp.stack(gain_grads, axis=1))[:2], axis=1
            )
            qkv_away, gain_all, gradient = tie(qkv_dot(1 - core, BF), gain_all, gradient)
            qkv_got = swap(jnp.concatenate([qkv_away, gain_all], axis=1), "col", 1)
            early = jnp.concatenate([pending, attn_last], axis=1)
            qkv_own = jnp.concatenate([qkv_dot(core, F32), gain_all.astype(F32)], axis=1)
            qkv_sum = qkv_own + qkv_got.astype(F32)
            gap = -qkv_sum.shape[1] % 128
            qkv_sum = jnp.concatenate(
                [qkv_sum, jnp.zeros((D, gap), F32), out_sum.astype(F32)], axis=1
            )
            out_begin = qkv_sum.shape[1] - q_width
            qkv_sum = reduce_rows(qkv_sum)
            ff_total = reduce_rows(ff_part).astype(BF)
            ff_total, gradient, *early = tie(ff_total, gradient, *dp_first(early))
            ff_total = dp_gather(ff_total)
            early = dp_second(early)
            first_total = dp_gather(qkv_sum.astype(BF))
            last_total, middle_total = early[:, :, :ff_width], early[:, :, ff_width:]
    input_grad = from_tokens(gradient.astype(BF), length).astype(F32)

    def in_order(parts):
        return [
            lax.dynamic_index_in_dim(parts, place(core, replica ^ i), 0, keepdims=False)
            for i in range(replicas)
        ]

    ff_totals = [in_order(ff_total), in_order(last_total)]

    def ff_of(number, begin, end):
        return jnp.concatenate([p[:, begin:end] for p in ff_totals[number]], axis=1).astype(F32)

    def total_of(parts):
        parts = parts.astype(F32)
        return (parts[0] + parts[3]) + (parts[1] + parts[2])

    first_total, middle_total = total_of(first_total), total_of(middle_total)
    attn_whole = [
        jnp.concatenate([first_total[:, :qkv_col], first_total[:, out_begin:]], axis=1),
        middle_total,
    ]

    def attn_of(number, begin, end):
        return attn_whole[number][:, begin:end]

    def stack(function):
        return jnp.stack([function(number) for number in range(layers)])

    gain_total = first_total[:, qkv_col : qkv_col + 4 * layers]
    gain_total = gain_total[:, : 2 * layers] + gain_total[:, 2 * layers :]
    gain_total = gain_total.T.reshape(layers, 2, -1)

    return (
        outputs,
        input_grad,
        gain_total[:, 0],
        stack(lambda n: attn_of(n, 0, q_width)),
        stack(lambda n: attn_of(n, q_width, q_width + k_width)),
        stack(lambda n: attn_of(n, q_width + k_width, qkv_col)),
        stack(lambda n: attn_of(n, qkv_col, a_col).T),
        gain_total[:, 1],
        stack(lambda n: ff_of(n, 0, f_part)),
        stack(lambda n: ff_of(n, f_part, 2 * f_part)),
        stack(lambda n: ff_of(n, 2 * f_part, ff_width).T),
    )


def solution(mesh):
    return jax.shard_map(
        shards,
        mesh=mesh,
        in_specs=(
            P("row", ("dp", "col")),
            P("row", ("dp", "col")),
            P(("dp", "row")),
            P(("dp", "row")),
            P(None, "row"),
            P(None, "row", "col"),
            P(None, "row", "col"),
            P(None, "row", "col"),
            P(None, "col", "row"),
            P(None, "row"),
            P(None, "row", "col"),
            P(None, "row", "col"),
            P(None, "col", "row"),
        ),
        out_specs=(
            P("row", ("dp", "col")),
            P("row", ("dp", "col")),
            P(None, "row"),
            P(None, "row", "col"),
            P(None, "row", "col"),
            P(None, "row", "col"),
            P(None, "col", "row"),
            P(None, "row"),
            P(None, "row", "col"),
            P(None, "row", "col"),
            P(None, "col", "row"),
        ),
        check_vma=False,
    )
```
